128 devices in a mesh: dp: 64 (over x, z_lo, y, core), tensor: 2 (over z_hi).
Axes of the slice: x: 4, y: 4, z: 4 (z_hi: 2, z_lo: 2; z = z_hi * 2 + z_lo), core: 2. Of those that a mesh axis runs over, the one named last changes fastest.
Arguments:
- inputs: bfloat16 [256, 197, 768], P(('dp', 'tensor')), may hold values from -6 to 6
- image_counts: int32 [64], P('dp'), may hold values from 1 to 4, as said below
- first_gain: float32 [768], replicated, may hold values from 0.5 to 1.5
- first_shift: float32 [768], replicated, may hold values from -1.5 to 1.5
- project_weight: bfloat16 [768, 3, 768], P(None, None, 'tensor'), may hold values from -0.21875 to 0.21875
- project_bias: float32 [2, 768], P(None, 'tensor'), may hold values from -1.5 to 1.5
- output_weight: bfloat16 [768, 768], P('tensor'), may hold values from -0.625 to 0.625
- output_bias: float32 [768], replicated, may hold values from -1.5 to 1.5
- second_gain: float32 [768], replicated, may hold values from 0.5 to 1.5
- second_shift: float32 [768], replicated, may hold values from -1.5 to 1.5
- expand_weight: bfloat16 [768, 3072], P(None, 'tensor'), may hold values from -0.21875 to 0.21875
- expand_bias: float32 [3072], P('tensor'), may hold values from -1.5 to 1.5
- reduce_weight: bfloat16 [3072, 768], P('tensor'), may hold values from -0.109375 to 0.109375
- reduce_bias: float32 [768], replicated, may hold values from -1.5 to 1.5
- out_cotangent: bfloat16 [256, 197, 768], P(('dp', 'tensor')), may hold values from -6 to 6
Outputs:
- block_out: bfloat16 [256, 197, 768], P(('dp', 'tensor'))
- input_grad: float32 [256, 197, 768], P(('dp', 'tensor'))
- grad_first_gain: float32 [768], replicated
- grad_first_shift: float32 [768], replicated
- grad_project_weight: float32 [768, 3, 768], P(None, None, 'tensor')
- grad_project_bias: float32 [2, 768], P(None, 'tensor')
- grad_output_weight: float32 [768, 768], P('tensor')
- grad_output_bias: float32 [768], replicated
- grad_second_gain: float32 [768], replicated
- grad_second_shift: float32 [768], replicated
- grad_expand_weight: float32 [768, 3072], P(None, 'tensor')
- grad_expand_bias: float32 [3072], P('tensor')
- grad_reduce_weight: float32 [3072, 768], P('tensor')
- grad_reduce_bias: float32 [768], replicated
The draws below stay inside these ranges and needn't reach their ends.
Inputs may be any that keep to these rules, and one draw needn't show every extreme that they name: image_counts[i] live images fill the first slots of dp device i's 4; the rest are padding; in every draw some device is full.
All inputs are finite; a program needn't handle non-finite values.
Results may differ from the reference program's by a relative error of at most 0.014.
Values may be sent and summed in bfloat16 or wider, within the bound.
A program may use at most 192 MiB of HBM per device.

```python
import jax
import jax.numpy as jnp
from jax import lax

D = 768
HEADS = 12
HD = 64
FF = 3072
S = 197
SLOTS = 4
IMG = 256
N_DP = 64


def draw_image_counts(key, part):
    key = jax.random.fold_in(key, 7)
    lower_key, upper_key, fullest_key = jax.random.split(key, 3)
    lower_draw = jax.random.randint(lower_key, (N_DP,), 1, SLOTS + 1)
    upper_draw = jax.random.randint(upper_key, (N_DP,), 2, SLOTS + 1)
    fullest = jax.random.randint(fullest_key, (), 0, N_DP)
    positions = jnp.arange(N_DP)
    return jnp.where(positions == fullest, SLOTS, jnp.minimum(lower_draw, upper_draw)).astype(jnp.int32)


def levels(own_key, extent, shards, least, top_value):
    factor_of, own = 1.0, jax.random.fold_in(own_key, 6)
    for axis_at, parts in shards:
        heights = jnp.exp(jax.random.uniform(jax.random.fold_in(own, axis_at), (parts,), jnp.float32, least / len(shards), top_value / len(shards)))
        factor_of = factor_of * jnp.repeat(heights, extent[axis_at] // parts).reshape([-1 if axis == axis_at else 1 for axis in range(len(extent))])
    return factor_of


def scatter_about(key, shape, deviation, reach, cuts=(), kind=jnp.bfloat16):
    factor_of = levels(key, shape, cuts, -0.22, 0.18) if cuts else 1.0
    values = jax.random.normal(key, shape, jnp.float32) * deviation * factor_of
    return jnp.minimum(jnp.maximum(values, -reach), reach).astype(kind)


def setup_inputs(seed: int = 0) -> dict:
    splits = jax.random.split(jax.random.key(seed), 16)
    return {
        "inputs": scatter_about(splits[0], (IMG, S, D), 1.0, 6.0, ((0, 128),)),
        "image_counts": draw_image_counts(jax.random.fold_in(splits[15], 71), 0),
        "first_gain": jnp.clip(1.0 + 0.1 * jax.random.normal(splits[2], (D,), jnp.float32), 0.5, 1.5),
        "first_shift": scatter_about(splits[3], (D,), 0.3, 1.5, (), jnp.float32),
        "project_weight": scatter_about(splits[4], (D, 3, D), D ** -0.5, 0.21875, ((2, 2),)),
        "project_bias": scatter_about(splits[5], (2, D), 0.3, 1.5, ((1, 2),), jnp.float32),
        "output_weight": scatter_about(splits[6], (D, D), (D // 8) ** -0.5, 0.625, ((0, 2),)),
        "output_bias": scatter_about(splits[7], (D,), 0.3, 1.5, (), jnp.float32),
        "second_gain": jnp.clip(1.0 + 0.1 * jax.random.normal(splits[8], (D,), jnp.float32), 0.5, 1.5),
        "second_shift": scatter_about(splits[9], (D,), 0.3, 1.5, (), jnp.float32),
        "expand_weight": scatter_about(splits[10], (D, FF), D ** -0.5, 0.21875, ((1, 2),)),
        "expand_bias": scatter_about(splits[11], (FF,), 0.3, 1.5, ((0, 2),), jnp.float32),
        "reduce_weight": scatter_about(splits[12], (FF, D), FF ** -0.5, 0.109375, ((0, 2),)),
        "reduce_bias": scatter_about(splits[13], (D,), 0.3, 1.5, (), jnp.float32),
        "out_cotangent": scatter_about(splits[14], (IMG, S, D), 1.0, 6.0, ((0, 128),)),
    }


@jax.custom_vjp
def low(v):
    return lax.optimization_barrier(v.astype(jnp.bfloat16)).astype(jnp.float32)

@jax.custom_vjp
def low_back(v):
    return v

def low_keep(v):
    return (low(v), None)

def low_pass(kept, grad):
    return (grad,)

def back_keep(v):
    return (v, None)

def back_low(kept, grad):
    return (low(grad),)
low.defvjp(low_keep, low_pass)
low_back.defvjp(back_keep, back_low)
EPSILON = 1e-06
HIGHEST = lax.Precision.HIGHEST

def layer_norm(stream, gain, shift):
    center = lax.optimization_barrier(jnp.mean(stream, axis=-1, keepdims=True))
    centered = stream - center
    spread = lax.optimization_barrier(jnp.mean(centered * centered, axis=-1, keepdims=True))
    return centered * lax.rsqrt(spread + EPSILON) * gain + shift

def forward(weights, stream, keeping):
    first_gain, first_shift, project_weight, project_bias, output_weight, output_bias, second_gain, second_shift, expand_weight, expand_bias, reduce_weight, reduce_bias = weights
    images = stream.shape[0]
    head_shape = (images, S, HEADS, HD)
    normed = low(layer_norm(stream, first_gain, first_shift))
    projected = jnp.einsum('gsd,dce->gsce', normed, project_weight, precision=HIGHEST)
    queries = low(low_back(projected[:, :, 0] + project_bias[0])).reshape(head_shape)
    key_rows = low(low_back(projected[:, :, 1])).reshape(head_shape)
    values = low(low_back(projected[:, :, 2] + project_bias[1])).reshape(head_shape)
    scores = low_back(jnp.einsum('gqhd,gkhd->ghqk', queries, key_rows, precision=HIGHEST) * HD ** (-0.5))
    soft_low = low(jax.nn.softmax(scores, axis=-1))
    head_mixed = jnp.einsum('ghqk,gkhd->gqhd', soft_low, values, precision=HIGHEST).reshape(images, S, D)
    head_mixed = low(low_back(head_mixed))
    attended = low_back(jnp.einsum('gsh,hd->gsd', head_mixed, output_weight, precision=HIGHEST) + output_bias)
    resid = stream + attended
    normed_two = low(layer_norm(resid, second_gain, second_shift))
    hidden = low_back(jnp.einsum('gsd,df->gsf', normed_two, expand_weight, precision=HIGHEST) + expand_bias)
    active = low(jax.nn.gelu(hidden, approximate=False))
    result = resid + jnp.einsum('gsf,fd->gsd', active, reduce_weight, precision=HIGHEST) + reduce_bias
    return result * keeping[:, None, None]

def reference(inputs, image_counts, first_gain, first_shift, project_weight, project_bias, output_weight, output_bias, second_gain, second_shift, expand_weight, expand_bias, reduce_weight, reduce_bias, out_cotangent):
    weights = tuple((entry.astype(jnp.float32) for entry in (first_gain, first_shift, project_weight, project_bias, output_weight, output_bias, second_gain, second_shift, expand_weight, expand_bias, reduce_weight, reduce_bias)))
    slot_index = jnp.arange(IMG, dtype=jnp.int32)
    owners = slot_index // SLOTS
    keeping = (slot_index % SLOTS < image_counts[owners]).astype(jnp.float32)
    step_devices = 4 if N_DP % 4 == 0 else 1
    step_images = SLOTS * step_devices
    blocks_count = IMG // step_images
    input_blocks = inputs.reshape(blocks_count, step_images, S, D)
    grad_blocks = out_cotangent.reshape(blocks_count, step_images, S, D)
    keep_blocks = keeping.reshape(blocks_count, step_images)

    def advance(totals, block_data):
        block_in, block_grad, block_keep = block_data
        outcome, pullback = jax.vjp(lambda weights_all, stream: forward(weights_all, stream, block_keep), weights, block_in.astype(jnp.float32))
        grad_weights, grad_stream = pullback(block_grad.astype(jnp.float32))
        return (jax.tree.map(jnp.add, totals, grad_weights), (outcome.astype(jnp.bfloat16), grad_stream))
    totals, (outcomes, grad_streams) = lax.scan(advance, jax.tree.map(jnp.zeros_like, weights), (input_blocks, grad_blocks, keep_blocks))
    return (outcomes.reshape(IMG, S, D), grad_streams.reshape(IMG, S, D), totals[0], totals[1], totals[2], totals[3], totals[4], totals[5], totals[6], totals[7], totals[8], totals[9], totals[10], totals[11])
```

```python
import functools

import jax
import jax.numpy as jnp
from jax import lax
from jax.experimental import pallas as pl
from jax.experimental.pallas import tpu as pltpu
from jax.sharding import PartitionSpec as P

HD = 64
EPSILON = 1e-06
TOKENS = 197
ROWS = 208
BOTH = 2 * ROWS
WIDTH = 768
HALF = 384
PAIRS = 6
BLOCK = 48
MESH = pl.DeviceIdType.MESH
F32 = jnp.float32
BF16 = jnp.bfloat16
ANY = pl.BlockSpec(memory_space=pl.ANY)
VMEM = pl.BlockSpec(memory_space=pltpu.VMEM)
SMEM = pl.BlockSpec(memory_space=pltpu.SMEM)


class Place:
    def __init__(self):
        dp = lax.axis_index("dp")
        self.dp = dp
        self.t = lax.axis_index("tensor")
        self.c = lax.rem(dp, 2)
        self.y = lax.rem(lax.div(dp, 2), 4)
        self.zl = lax.rem(lax.div(dp, 8), 2)
        self.x = lax.div(dp, 16)
        self.z = self.t * 2 + self.zl

    def at(self, x=None, y=None, z=None, c=None):
        x = self.x if x is None else x
        y = self.y if y is None else y
        z = self.z if z is None else z
        c = self.c if c is None else c
        return (((x * 2 + lax.rem(z, 2)) * 4 + y) * 2 + c, lax.div(z, 2))

    def neighbours(self):
        return [
            self.at(c=1 - self.c),
            self.at(x=up(self.x)),
            self.at(x=down(self.x)),
            self.at(y=up(self.y)),
            self.at(y=down(self.y)),
            self.at(z=up(self.z)),
            self.at(z=down(self.z)),
        ]


def up(v):
    return lax.rem(v + 1, 4)


def down(v):
    return lax.rem(v + 3, 4)


def across(v):
    return lax.rem(v + 2, 4)


class Post:
    def __init__(self, send_sems, recv_sems):
        self.send_sems, self.recv_sems, self.copies = send_sems, recv_sems, []

    def describe(self, src, dst, device, k):
        return pltpu.make_async_remote_copy(
            src_ref=src,
            dst_ref=dst,
            send_sem=self.send_sems.at[k],
            recv_sem=self.recv_sems.at[k],
            device_id=device,
            device_id_type=MESH,
        )

    def send(self, src, dst, device):
        copy = self.describe(src, dst, device, len(self.copies))
        copy.start()
        self.copies.append(copy)
        return copy

    def drain(self):
        for copy in self.copies:
            copy.wait_send()


def greet(devices):
    barrier = pltpu.get_barrier_semaphore()
    for device in devices:
        pl.semaphore_signal(barrier, inc=1, device_id=device, device_id_type=MESH)
    pl.semaphore_wait(barrier, len(devices))


def gather_blocks(me, post, out):
    x, y, zl, c = me.x, me.y, me.zl, me.c
    xr, xl, xo = up(x), down(x), across(x)
    yr, yl, yo = up(y), down(y), across(y)
    zo = 1 - zl
    to_xr, to_xl = me.at(x=xr), me.at(x=xl)
    to_yr, to_yl = me.at(y=yr), me.at(y=yl)
    to_z = me.at(z=me.t * 2 + zo)
    to_c = me.at(c=1 - c)

    def put(ref, device):
        return post.send(ref, ref, device)

    a, b, d = out.at[0], out.at[1], out.at[2]
    own_a, own_b, own_d = a.at[x, zl, y, c], b.at[x, zl, y, c], d.at[x, zl, y, c]
    a1 = put(own_a, to_z)
    b1r, b1l = put(own_b, to_xr), put(own_b, to_xl)
    d1r, d1l = put(own_d, to_yr), put(own_d, to_yl)
    b1r.wait_recv()
    b1f = put(b.at[xl, zl, y, c], to_xr)
    d1l.wait_recv()
    d1f = put(d.at[x, zl, yr, c], to_yl)
    a1.wait_recv()
    row_a = a.at[x, :, y, c]
    a2r, a2l = put(row_a, to_yr), put(row_a, to_yl)
    b1l.wait_recv()
    b1f.wait_recv()
    b2 = put(b.at[:, zl, y, c], to_z)
    d1r.wait_recv()
    d1f.wait_recv()
    row_d = d.at[x, zl, :, c]
    d2r, d2l = put(row_d, to_xr), put(row_d, to_xl)
    d3 = [put(row_d, to_z)]
    dc = [put(row_d, to_c)]
    a2r.wait_recv()
    a2fr = put(a.at[x, 0, yl, c], to_yr)
    a2l.wait_recv()
    a2fl = put(a.at[x, 1, yr, c], to_yl)
    b2.wait_recv()
    row_b = b.at[:, :, y, c]
    b3r, b3l = put(row_b, to_yr), put(row_b, to_yl)
    bc = [put(row_b, to_c)]
    a2fr.wait_recv()
    a2fl.wait_recv()
    row_a = a.at[x, :, :, c]
    a3r, a3l = put(row_a, to_xr), put(row_a, to_xl)
    ac = [put(row_a, to_c)]
    d2r.wait_recv()
    d2fr = put(d.at[xl, zl, 0:2, c], to_xr)
    d2l.wait_recv()
    d2fl = put(d.at[xr, zl, 2:4, c], to_xl)
    d3.append(put(d.at[xl, zl, :, c], to_z))
    dc.append(put(d.at[xl, zl, :, c], to_c))
    d3.append(put(d.at[xr, zl, :, c], to_z))
    dc.append(put(d.at[xr, zl, :, c], to_c))
    d2fr.wait_recv()
    d2fl.wait_recv()
    d3.append(put(d.at[xo, zl, :, c], to_z))
    dc.append(put(d.at[xo, zl, :, c], to_c))
    b3r.wait_recv()
    b3fr = put(b.at[:, 0, yl, c], to_yr)
    bc.append(put(b.at[:, :, yl, c], to_c))
    b3l.wait_recv()
    b3fl = put(b.at[:, 1, yr, c], to_yl)
    bc.append(put(b.at[:, :, yr, c], to_c))
    a3r.wait_recv()
    a3fr = put(a.at[xl, 0, :, c], to_xr)
    ac.append(put(a.at[xl, :, :, c], to_c))
    a3l.wait_recv()
    a3fl = put(a.at[xr, 1, :, c], to_xl)
    ac.append(put(a.at[xr, :, :, c], to_c))
    for copy, xs in zip(d3, (x, xl, xr, xo)):
        copy.wait_recv()
        dc.append(put(d.at[xs, zo, :, c], to_c))
    a3fr.wait_recv()
    a3fl.wait_recv()
    ac.append(put(a.at[xo, :, :, c], to_c))
    b3fr.wait_recv()
    b3fl.wait_recv()
    bc.append(put(b.at[:, :, yo, c], to_c))
    for copy in ac + bc + dc:
        copy.wait_recv()


GATHER_COPIES = 5 + 2 + 2 + 1 + 2 + 2 + 2 + 2 + 2 + 4 + 2 + 2 + 4 + 4 + 8


def weights_kernel(project, output, expand, reduce, small, out, small_out, send_sems, recv_sems):
    me = Place()
    partner = me.at(z=across(me.z))
    greet(me.neighbours() + [partner])
    post = Post(send_sems, recv_sems)
    dp = me.dp
    place = (me.x, me.zl, me.y, me.c)
    slots = [out.at[(part, *place)] for part in range(3)]

    copies = [post.describe(slots[0], slots[0], partner, 0)]
    post.copies.append(copies[0])

    @pl.when(dp < 48)
    def _():
        rows = pl.multiple_of(lax.rem(dp, 16) * BLOCK, BLOCK)
        post.describe(
            project.at[lax.div(dp, 16), pl.ds(rows, BLOCK), :], slots[0], partner, 0
        ).start()

    @pl.when(dp >= 48)
    def _():
        spot = dp - 48
        rows = pl.multiple_of(lax.rem(spot, 8) * BLOCK, BLOCK)
        cols = pl.multiple_of(lax.div(spot, 8) * HALF, HALF)
        post.describe(
            output.at[pl.ds(rows, BLOCK), pl.ds(cols, HALF)], slots[0], partner, 0
        ).start()

    rows = pl.multiple_of(lax.rem(dp, 16) * BLOCK, BLOCK)
    cols = pl.multiple_of(lax.div(dp, 16) * HALF, HALF)
    copies.append(post.send(expand.at[pl.ds(rows, BLOCK), pl.ds(cols, HALF)], slots[1], partner))
    rows = pl.multiple_of(lax.rem(dp, 32) * BLOCK, BLOCK)
    cols = pl.multiple_of(lax.div(dp, 32) * HALF, HALF)
    copies.append(post.send(reduce.at[pl.ds(rows, BLOCK), pl.ds(cols, HALF)], slots[2], partner))
    small_copy = post.send(small, small_out, partner)
    for copy in copies:
        copy.wait_recv()
    gather_blocks(me, post, out)
    small_copy.wait_recv()
    post.drain()


def other_weights(project, output, expand, reduce, small):
    count = GATHER_COPIES + 4
    return pl.pallas_call(
        weights_kernel,
        out_shape=(
            jax.ShapeDtypeStruct((3, 4, 2, 4, 2, BLOCK, HALF), BF16),
            jax.ShapeDtypeStruct(small.shape, F32),
        ),
        in_specs=[ANY] * 4 + [VMEM],
        out_specs=(ANY, VMEM),
        scratch_shapes=[pltpu.SemaphoreType.DMA((count,)), pltpu.SemaphoreType.DMA((count,))],
        compiler_params=pltpu.CompilerParams(collective_id=0, has_side_effects=True),
        name="weights_gather",
    )(project, output, expand, reduce, small)


def add_blocks(count, target, sources):
    def step(k, carry):
        ref = target(k)
        total = ref[...].astype(F32)
        for source in sources:
            total = total + source(k)[...].astype(F32)
        ref[...] = total.astype(BF16)
        return carry

    lax.fori_loop(0, count, step, 0)


class Ring:
    def __init__(self, post, me, right, left, view, blocks, block_of, bufs):
        self.post, self.me, self.right, self.left = post, me, right, left
        self.view, self.blocks, self.block_of = view, blocks, block_of
        self.relay_l, self.relay_r, self.left_a, self.left_b, self.right_a, self.right_b = bufs

    def add(self, half, d, bufs):
        ref = self.view(half, d)
        if self.blocks[half] is None:
            total = ref[...].astype(F32)
            for buf in bufs:
                total = total + buf[...].astype(F32)
            ref[...] = total.astype(BF16)
        else:
            add_blocks(
                self.blocks[half],
                lambda k: self.block_of(ref, k),
                [lambda k, buf=buf: self.block_of(buf, k) for buf in bufs],
            )

    def start_far(self):
        far = across(self.me)
        self.far_r = self.post.send(self.view(0, far), self.relay_l, self.right)
        self.far_l = self.post.send(self.view(1, far), self.relay_r, self.left)

    def start_near(self):
        self.near_r = self.post.send(self.view(1, up(self.me)), self.left_b, self.right)
        self.near_l = self.post.send(self.view(0, down(self.me)), self.right_a, self.left)

    def relay(self):
        self.far_r.wait_recv()
        self.add(0, up(self.me), [self.relay_l])
        self.last_r = self.post.send(self.view(0, up(self.me)), self.left_a, self.right)
        self.far_l.wait_recv()
        self.add(1, down(self.me), [self.relay_r])
        self.last_l = self.post.send(self.view(1, down(self.me)), self.right_b, self.left)

    def finish(self):
        self.near_r.wait_recv()
        self.near_l.wait_recv()
        self.last_r.wait_recv()
        self.add(0, self.me, [self.left_a, self.right_a])
        self.last_l.wait_recv()
        self.add(1, self.me, [self.left_b, self.right_b])


def sum_kernel(grads, small, out, small_out, mine, theirs, big, mid, low, acc, arrived, own_sems, send_sems, recv_sems):
    me = Place()
    greet(me.neighbours())
    post = Post(send_sems, recv_sems)
    x, y, z, zl, c, t = me.x, me.y, me.z, me.zl, me.c, me.t
    to_c = me.at(c=1 - c)
    rings = {
        "x": (x, me.at(x=up(x)), me.at(x=down(x))),
        "y": (y, me.at(y=up(y)), me.at(y=down(y))),
        "z": (z, me.at(z=up(z)), me.at(z=down(z))),
    }

    def side(d):
        return lax.rem(lax.div(d, 2) + t, 2)

    def chunk(ref, part, d):
        if part == 0:
            return ref.at[:, 0, d]
        if part == 1:
            return ref.at[:, 1, :, :, d]
        return ref.at[side(d), 2, :, lax.rem(d, 2)]

    def chunk_block(ref, part, k):
        if part == 0:
            return ref.at[lax.div(k, 8), lax.rem(lax.div(k, 4), 2), lax.rem(k, 4)]
        if part == 1:
            return ref.at[lax.div(k, 8), lax.rem(lax.div(k, 2), 4), lax.rem(k, 2)]
        return ref.at[lax.div(k, 4), lax.rem(k, 4)]

    partners = [
        to_c,
        me.at(x=x + 1 - 2 * lax.rem(x, 2)),
        me.at(x=3 - x),
        me.at(y=y + 1 - 2 * lax.rem(y, 2)),
        me.at(y=3 - y),
        me.at(z=z + 1 - 2 * lax.rem(z, 2)),
        me.at(z=3 - z),
    ]
    acc[0] = small[...]
    state = {"step": 0, "copy": None}

    def small_send():
        k = state["step"]
        state["copy"] = post.send(acc.at[k], arrived.at[k], partners[k])

    def small_next():
        k = state["step"]
        state["copy"].wait_recv()
        acc[k + 1] = acc[k] + arrived[k]
        state["step"] = k + 1
        if k + 1 < 7:
            small_send()

    small_send()

    kinds = [across, up, down, lambda v: v]
    order = [(part, kind) for kind in range(4) for part in range(3)]
    where = [x, y, z]
    core = {}
    for n, (part, kind) in enumerate(order):
        d = kinds[kind](where[part])
        src, dst = chunk(grads, part, d), chunk(theirs, part, d)
        if part == 0:
            there, here = src.at[..., 1 - c, :, :], src.at[..., c, :, :]
        else:
            there, here = src.at[..., 1 - c, :, :], src.at[..., c, :, :]
        local = pltpu.make_async_copy(here, chunk(mine, part, d), own_sems.at[n])
        local.start()
        core[part, kind] = (post.send(there, dst, to_c), local)

    def settle(part, kind):
        d = kinds[kind](where[part])
        remote, local = core[part, kind]
        local.wait()
        remote.wait_recv()
        target, source = chunk(mine, part, d), chunk(theirs, part, d)
        add_blocks(
            16,
            lambda k: chunk_block(target, part, k),
            [lambda k: chunk_block(source, part, k)],
        )

    def first_view(part):
        def view(half, d):
            ref = chunk(mine, part, d)
            if part == 2:
                return ref.at[pl.ds(2 * half, 2)]
            return ref.at[half]

        return view

    def first_block(part):
        if part == 0:
            return lambda ref, k: ref.at[lax.div(k, 4), lax.rem(k, 4)]
        if part == 1:
            return lambda ref, k: ref.at[lax.div(k, 2), lax.rem(k, 2)]
        return lambda ref, k: ref.at[lax.div(k, 4), lax.rem(k, 4)]

    def big_bufs(part):
        shapes = [(2, 4), (4, 2), (2, 4)]
        return [big[part].at[i] for i in range(6)]

    stage = [
        Ring(post, *rings["xyz"[part]], first_view(part), (8, 8), first_block(part), big_bufs(part))
        for part in range(3)
    ]
    for part in range(3):
        settle(part, 0)
        stage[part].start_far()
    small_next()
    for part in range(3):
        settle(part, 1)
        settle(part, 2)
        stage[part].start_near()
    small_next()
    for part in range(3):
        stage[part].relay()
    small_next()
    for part in range(3):
        settle(part, 3)

    def second_view(part):
        def view(half, d):
            if part == 0:
                return mine.at[half, 0, x, :, d]
            if part == 1:
                return mine.at[side(d), 1, pl.ds(2 * half, 2), lax.rem(d, 2), y]
            return mine.at[0, 2, d, zl, pl.ds(2 * half, 2)]

        return view

    second = []
    for part in range(3):
        stage[part].finish()
        ring = Ring(
            post,
            *rings["yzx"[part]],
            second_view(part),
            (2, 2),
            lambda ref, k: ref.at[k],
            [mid.at[part, i] for i in range(6)],
        )
        ring.start_far()
        ring.start_near()
        second.append(ring)
    small_next()
    for ring in second:
        ring.relay()
    small_next()

    def third_view(part):
        def view(half, d):
            rows = pl.ds(0, 32) if half == 0 else pl.ds(32, 16)
            if part == 0:
                return mine.at[side(d), 0, x, lax.rem(d, 2), y, rows]
            if part == 1:
                return mine.at[0, 1, d, zl, y, rows]
            return mine.at[0, 2, x, zl, d, rows]

        return view

    third = []
    for part in range(3):
        second[part].finish()
        bufs = [
            low.at[part, i, pl.ds(0, 32) if half == 0 else pl.ds(32, 16)]
            for i, half in enumerate((0, 1, 0, 1, 0, 1))
        ]
        ring = Ring(post, *rings["zxy"[part]], third_view(part), (None, None), None, bufs)
        ring.start_far()
        ring.start_near()
        third.append(ring)
    small_next()
    for ring in third:
        ring.relay()
    small_next()
    small_out[...] = acc[7]
    locals_ = []
    for part in range(3):
        third[part].finish()
        local = pltpu.make_async_copy(
            mine.at[0, part, x, zl, y], out.at[part, x, zl, y, c], own_sems.at[12 + part]
        )
        local.start()
        locals_.append(local)
    for local in locals_:
        local.wait()
    gather_blocks(me, post, out)
    post.drain()


SUM_COPIES = 7 + 12 + 3 * 3 * 6


def summed_grads(grads, small):
    count = GATHER_COPIES + SUM_COPIES
    block = (BLOCK, HALF)
    first_shapes = [(6, 2, 4), (6, 4, 2), (6, 2, 4)]

    def kernel(g, s, out, s_out, mine, theirs, big0, big1, big2, *rest):
        sum_kernel(g, s, out, s_out, mine, theirs, (big0, big1, big2), *rest)

    return pl.pallas_call(
        kernel,
        out_shape=(
            jax.ShapeDtypeStruct((3, 4, 2, 4, 2, *block), BF16),
            jax.ShapeDtypeStruct(small.shape, F32),
        ),
        in_specs=[ANY, VMEM],
        out_specs=(ANY, VMEM),
        scratch_shapes=[
            pltpu.VMEM((2, 3, 4, 2, 4, *block), BF16),
            pltpu.VMEM((2, 3, 4, 2, 4, *block), BF16),
            *[pltpu.VMEM((*shape, *block), BF16) for shape in first_shapes],
            pltpu.VMEM((3, 6, 2, *block), BF16),
            pltpu.VMEM((3, 6, *block), BF16),
            pltpu.VMEM((8, *small.shape), F32),
            pltpu.VMEM((7, *small.shape), F32),
            pltpu.SemaphoreType.DMA((15,)),
            pltpu.SemaphoreType.DMA((count,)),
            pltpu.SemaphoreType.DMA((count,)),
        ],
        compiler_params=pltpu.CompilerParams(
            collective_id=1, has_side_effects=True, vmem_limit_bytes=40 << 20
        ),
        name="gradient_sum",
    )(grads, small)


def dot(a, b, dims=((1,), (0,))):
    return lax.dot_general(a, b, (dims, ((), ())), preferred_element_type=F32)


NT = ((1,), (1,))
TN = ((0,), (0,))


def phi_terms(h):
    v = h * 0.7071067811865476
    v = jnp.clip(v, -3.7439211627767994, 3.7439211627767994)
    s = v * v
    top = 0.00022905065861350646
    for k in (0.0034082910107109506, 0.050955695062380861, 0.18520832239976145, 1.128379143519084):
        top = top * s + k
    low = -1.1791602954361697e-7
    for k in (
        0.000023547966471313185,
        0.0010179625278914885,
        0.014070470171167667,
        0.11098505178285362,
        0.49746925110067538,
        1.0,
    ):
        low = low * s + k
    big = 0.5 + 0.5 * (v * top / low)
    small = jnp.exp(h * h * -0.5) * 0.3989422804014327
    return big, big + h * small


def norm_stats(v):
    center = jnp.mean(v, axis=-1, keepdims=True)
    centered = v - center
    spread = jnp.mean(centered * centered, axis=-1, keepdims=True)
    scale = lax.rsqrt(spread + EPSILON)
    return centered * scale, scale


def row_loop(step, rows=16):
    def body(k, carry):
        step(pl.ds(pl.multiple_of(k * rows, rows), rows))
        return carry

    lax.fori_loop(0, BOTH // rows, body, 0)


def layer_kernel(
    counts,
    x_in,
    cot_in,
    vectors,
    small_mine,
    small_other,
    project,
    output,
    expand,
    reduce,
    other,
    block_out,
    input_grad,
    grads,
    small_out,
    w_qkv,
    w_out,
    w_expand,
    w_reduce,
    g_all,
    stream,
    resid,
    grad_resid,
    go,
    normed,
    normed_two,
    qkv,
    mixed,
    grad_mixed,
    probs,
    hidden,
    slope,
    active,
    grad_hidden,
    branch,
    dnorm,
    grad_attended,
    grad_qkv,
    sums,
    w_sems,
    g_sems,
):
    t = lax.axis_index("tensor")
    loads = []

    def load(src, dst):
        copy = pltpu.make_async_copy(src, dst, w_sems.at[len(loads)])
        copy.start()
        loads.append(copy)

    left, right = pl.ds(0, HALF), pl.ds(HALF, HALF)
    for j in range(3):
        load(project.at[j], w_qkv.at[j, :, left])
        load(other.at[0, pl.ds(j * WIDTH, WIDTH)], w_qkv.at[j, :, right])
    load(output, w_out.at[left])
    load(other.at[0, pl.ds(3 * WIDTH, HALF)], w_out.at[right, left])
    load(other.at[0, pl.ds(3 * WIDTH + HALF, HALF)], w_out.at[right, right])
    for j in range(2):
        load(expand.at[:, pl.ds(j * WIDTH, WIDTH)], w_expand.at[j])
        load(reduce.at[pl.ds(j * WIDTH, WIDTH)], w_reduce.at[j])
        for k, cols in enumerate((left, right)):
            load(other.at[1, pl.ds((2 * j + k) * WIDTH, WIDTH)], w_expand.at[2 + j, :, cols])
            load(
                other.at[2, pl.ds(k * 2 * WIDTH + j * WIDTH, WIDTH)],
                w_reduce.at[2 + j, :, cols],
            )

    stores = []

    def store(src, dst):
        copy = pltpu.make_async_copy(src, dst, g_sems.at[len(stores)])
        copy.start()
        stores.append(copy)

    live = counts[0] - 2 * t
    keep = [jnp.where(live > i, 1.0, 0.0) for i in range(2)]
    first_gain, first_shift = vectors[0:1], vectors[1:2]
    second_gain, second_shift = vectors[2:3], vectors[3:4]
    output_bias, reduce_bias = vectors[4:5], vectors[5:6]
    sums[...] = jnp.zeros_like(sums)

    def gather_sum(row, value):
        sums[pl.ds(row * 8, 8)] += value.reshape(-1, 8, WIDTH).sum(axis=0)

    def first_norm(rows):
        v = x_in[rows].astype(F32)
        n, _ = norm_stats(v)
        normed[rows] = (n * first_gain + first_shift).astype(BF16)

    row_loop(first_norm)
    for i in range(2):
        own = pl.ds(i * ROWS, ROWS)
        go[own] = (cot_in[own].astype(F32) * keep[i]).astype(BF16)

    for copy in loads[:6]:
        copy.wait()

    def project_step(j, carry):
        bias = jnp.concatenate([small_mine[pl.ds(j, 1)], small_other[pl.ds(j, 1)]], axis=1)
        result = (dot(normed[...], w_qkv[j]) + bias).astype(BF16)
        for p in range(PAIRS):
            qkv[j, p] = result[:, 128 * p : 128 * (p + 1)]
        return carry

    lax.fori_loop(0, 3, project_step, 0)

    lane = lax.broadcasted_iota(jnp.int32, (ROWS, 128), 1)
    first_head = lane < HD

    def split(pair):
        zero = jnp.zeros_like(pair)
        return jnp.concatenate(
            [jnp.where(first_head, pair, zero), jnp.where(first_head, zero, pair)], axis=0
        )

    def joined(both):
        return jnp.where(first_head, both[:ROWS], both[ROWS:])

    def image_rows(i):
        return pl.ds(pl.multiple_of(i * ROWS, 16), ROWS)

    key_dead = lax.broadcasted_iota(jnp.int32, (2 * ROWS, ROWS), 1) >= TOKENS

    def attend(k, carry):
        p, rows = lax.div(k, 2), image_rows(lax.rem(k, 2))
        queries = split(qkv[0, p, rows] * jnp.asarray(HD**-0.5, BF16))
        scores = dot(queries, qkv[1, p, rows], NT)
        scores = jnp.where(key_dead, -1e30, scores)
        raised = jnp.exp(scores - jnp.max(scores, axis=-1, keepdims=True))
        soft = raised / jnp.sum(raised, axis=-1, keepdims=True)
        probs[k] = soft
        mixed[p, rows] = joined(dot(soft.astype(BF16), qkv[2, p, rows])).astype(BF16)
        return carry

    lax.fori_loop(0, 2 * PAIRS, attend, 0)

    def all_pairs(ref):
        return jnp.concatenate([ref[p] for p in range(PAIRS)], axis=1)

    for copy in loads[6:9]:
        copy.wait()
    resid[...] = dot(all_pairs(mixed), w_out[...])

    def second_norm(rows):
        v = resid[rows] + x_in[rows].astype(F32) + output_bias
        resid[rows] = v
        n, _ = norm_stats(v)
        normed_two[rows] = (n * second_gain + second_shift).astype(BF16)

    row_loop(second_norm)

    for copy in loads[9:]:
        copy.wait()
    branch[...] = jnp.zeros_like(branch)
    dnorm[...] = jnp.zeros_like(dnorm)

    def feed(j, carry):
        o, jj = lax.div(j, 2), lax.rem(j, 2)
        at = 2 + 2 * jj
        bias_mine = jnp.concatenate([small_mine[pl.ds(at + 1, 1)], small_mine[pl.ds(at + 2, 1)]], axis=1)
        bias_other = jnp.concatenate([small_other[pl.ds(at + 1, 1)], small_other[pl.ds(at + 2, 1)]], axis=1)
        bias = jnp.where(o == 0, bias_mine, bias_other)
        hidden[...] = dot(normed_two[...], w_expand[j]) + bias

        def gelu(rows):
            h = hidden[rows]
            big, slope_rows = phi_terms(h)
            active[rows] = (h * big).astype(BF16)
            slope[rows] = slope_rows

        row_loop(gelu)
        branch[...] += dot(active[...], w_reduce[j])
        grad_active = dot(go[...], w_reduce[j], NT)
        gh = (grad_active * slope[...]).astype(BF16)
        grad_hidden[...] = gh
        sums[pl.ds(pl.multiple_of((8 + j) * 8, 8), 8)] = gh.astype(F32).reshape(-1, 8, WIDTH).sum(axis=0)
        dnorm[...] += dot(grad_hidden[...], w_expand[j], NT)
        grad = dot(normed_two[...], grad_hidden[...], TN).astype(BF16)
        start = pl.multiple_of(jj * 2 * WIDTH, WIDTH)
        g_all[o, 1, pl.ds(start, WIDTH)] = grad[:, :HALF]
        g_all[o, 1, pl.ds(start + WIDTH, WIDTH)] = grad[:, HALF:]
        grad = dot(active[...], go[...], TN).astype(BF16)
        start = pl.multiple_of(jj * WIDTH, WIDTH)
        g_all[o, 2, pl.ds(start, WIDTH)] = grad[:, :HALF]
        g_all[o, 2, pl.ds(start + 2 * WIDTH, WIDTH)] = grad[:, HALF:]
        return carry

    lax.fori_loop(0, 4, feed, 0)
    for o in range(2):
        store(g_all.at[o, pl.ds(1, 2)], grads.at[o, pl.ds(1, 2)])

    for i in range(2):
        own = pl.ds(i * ROWS, ROWS)
        block_out[own] = ((resid[own] + branch[own] + reduce_bias) * keep[i]).astype(BF16)

    def norm_back(n, scale, grad, gain):
        e = grad * gain
        return scale * (
            e - jnp.mean(e, axis=-1, keepdims=True) - n * jnp.mean(e * n, axis=-1, keepdims=True)
        )

    def second_back(rows):
        n, scale = norm_stats(resid[rows])
        grad = dnorm[rows]
        total = go[rows].astype(F32)
        gather_sum(5, total)
        total = total + norm_back(n, scale, grad, second_gain)
        grad_resid[rows] = total
        low = total.astype(BF16)
        grad_attended[rows] = low
        gather_sum(2, grad * n)
        gather_sum(3, grad)
        gather_sum(4, low.astype(F32))

    row_loop(second_back)

    grad = dot(all_pairs(mixed), grad_attended[...], TN).astype(BF16)
    for o in range(2):
        for k in range(2):
            g_all[o, 0, 3 * WIDTH + k * HALF : 3 * WIDTH + (k + 1) * HALF] = grad[
                o * HALF : (o + 1) * HALF, k * HALF : (k + 1) * HALF
            ]
    result = dot(grad_attended[...], w_out[...], NT).astype(BF16)
    for p in range(PAIRS):
        grad_mixed[p] = result[:, 128 * p : 128 * (p + 1)]

    def attend_back(k, carry):
        p, rows = lax.div(k, 2), image_rows(lax.rem(k, 2))
        grad_out = split(grad_mixed[p, rows])
        soft = probs[k]
        grad_soft = dot(grad_out, qkv[2, p, rows], NT)
        inner = jnp.sum(soft * grad_soft, axis=-1, keepdims=True)
        grad_scores = (soft * (grad_soft - inner)).astype(BF16)
        scale = jnp.asarray(HD**-0.5, BF16)
        queries = split(qkv[0, p, rows] * scale)
        grad_qkv[0, p, rows] = joined(dot(grad_scores, qkv[1, p, rows] * scale)).astype(BF16)
        grad_qkv[1, p, rows] = dot(grad_scores, queries, TN).astype(BF16)
        grad_qkv[2, p, rows] = dot(soft.astype(BF16), grad_out, TN).astype(BF16)
        return carry

    lax.fori_loop(0, 2 * PAIRS, attend_back, 0)

    dnorm[...] = jnp.zeros_like(dnorm)

    def project_back(j, carry):
        given = jnp.concatenate([grad_qkv[j, p] for p in range(PAIRS)], axis=1)
        grad = dot(normed[...], given, TN).astype(BF16)
        start = pl.multiple_of(j * WIDTH, WIDTH)
        g_all[0, 0, pl.ds(start, WIDTH)] = grad[:, :HALF]
        g_all[1, 0, pl.ds(start, WIDTH)] = grad[:, HALF:]
        dnorm[...] += dot(given, w_qkv[j], NT)
        part = given.astype(F32).reshape(-1, 8, WIDTH).sum(axis=0)
        row = jnp.where(j == 0, 6, jnp.where(j == 2, 7, 12))
        sums[pl.ds(pl.multiple_of(row * 8, 8), 8)] = part
        return carry

    lax.fori_loop(0, 3, project_back, 0)
    for o in range(2):
        store(g_all.at[o, 0], grads.at[o, 0])

    def first_back(rows):
        n, scale = norm_stats(x_in[rows].astype(F32))
        grad = dnorm[rows]
        input_grad[rows] = grad_resid[rows] + norm_back(n, scale, grad, first_gain)
        gather_sum(0, grad * n)
        gather_sum(1, grad)

    row_loop(first_back)

    totals = [jnp.sum(sums[8 * k : 8 * (k + 1)], axis=0, keepdims=True) for k in range(12)]
    first = t == 0

    def swapped(row):
        return jnp.where(first, row, jnp.concatenate([row[:, HALF:], row[:, :HALF]], axis=1))

    rows = totals[:6] + [swapped(totals[6]), swapped(totals[7])]
    for k in range(4):
        rows.append(jnp.where(first, totals[8 + k], totals[8 + (k + 2) % 4]))
    for k in range(12):
        small_out[k : k + 1] = rows[k]
    small_out[12:16] = jnp.zeros((4, WIDTH), F32)
    for copy in stores:
        copy.wait()


def layer(counts, x, cot, vectors, small_mine, small_other, weights, other):
    def buf(*shape, dtype=BF16):
        return pltpu.VMEM(shape, dtype)

    return pl.pallas_call(
        layer_kernel,
        out_shape=(
            jax.ShapeDtypeStruct((BOTH, WIDTH), BF16),
            jax.ShapeDtypeStruct((BOTH, WIDTH), F32),
            jax.ShapeDtypeStruct((2, 3, 4 * WIDTH, HALF), BF16),
            jax.ShapeDtypeStruct((16, WIDTH), F32),
        ),
        in_specs=[SMEM] + [VMEM] * 5 + [ANY] * 5,
        out_specs=(VMEM, VMEM, ANY, VMEM),
        scratch_shapes=[
            buf(3, WIDTH, WIDTH),
            buf(WIDTH, WIDTH),
            buf(4, WIDTH, WIDTH),
            buf(4, WIDTH, WIDTH),
            buf(2, 3, 4 * WIDTH, HALF),
            buf(8, 128, dtype=F32),
            buf(BOTH, WIDTH, dtype=F32),
            buf(BOTH, WIDTH, dtype=F32),
            buf(BOTH, WIDTH),
            buf(BOTH, WIDTH),
            buf(BOTH, WIDTH),
            buf(3, PAIRS, BOTH, 128),
            buf(PAIRS, BOTH, 128),
            buf(PAIRS, BOTH, 128),
            buf(2 * PAIRS, 2 * ROWS, ROWS, dtype=F32),
            buf(BOTH, WIDTH, dtype=F32),
            buf(BOTH, WIDTH, dtype=F32),
            buf(BOTH, WIDTH),
            buf(BOTH, WIDTH),
            buf(BOTH, WIDTH, dtype=F32),
            buf(BOTH, WIDTH, dtype=F32),
            buf(BOTH, WIDTH),
            buf(3, PAIRS, BOTH, 128),
            buf(13 * 8, WIDTH, dtype=F32),
            pltpu.SemaphoreType.DMA((24,)),
            pltpu.SemaphoreType.DMA((4,)),
        ],
        compiler_params=pltpu.CompilerParams(vmem_limit_bytes=62 << 20),
        name="layer",
    )(counts, x, cot, vectors, small_mine, small_other, *weights, other)


def shards(
    inputs,
    image_counts,
    first_gain,
    first_shift,
    project_weight,
    project_bias,
    output_weight,
    output_bias,
    second_gain,
    second_shift,
    expand_weight,
    expand_bias,
    reduce_weight,
    reduce_bias,
    out_cotangent,
):
    project = jnp.transpose(project_weight, (1, 0, 2))
    small = jnp.concatenate(
        [
            project_bias[0:1],
            jnp.zeros((1, HALF), F32),
            project_bias[1:2],
            expand_bias.reshape(4, HALF),
            jnp.zeros((1, HALF), F32),
        ]
    )
    weights = (project, output_weight, expand_weight, reduce_weight)
    other, small_other = other_weights(*weights, small)
    vectors = jnp.stack(
        [first_gain, first_shift, second_gain, second_shift, output_bias, reduce_bias, first_gain, first_gain]
    )

    def padded(array):
        return jnp.pad(array, ((0, 0), (0, ROWS - TOKENS), (0, 0))).reshape(BOTH, WIDTH)

    block_out, input_grad, grads, small_grads = layer(
        image_counts,
        padded(inputs),
        padded(out_cotangent),
        vectors,
        small,
        small_other,
        weights,
        other.reshape(3, 4 * WIDTH, HALF),
    )
    total, small_total = summed_grads(
        grads.reshape(2, 3, 4, 2, 4, 2, BLOCK, HALF), small_grads
    )
    total = total.reshape(3, 4 * WIDTH, HALF)
    t = lax.axis_index("tensor")

    def own_tokens(array):
        return array.reshape(2, ROWS, WIDTH)[:, :TOKENS]

    def side_by_side(array, count):
        rows = array.shape[0] // count
        return jnp.transpose(array.reshape(count, rows, HALF), (1, 0, 2)).reshape(
            rows, count * HALF
        )

    attention = total[0]
    project_grad = jnp.transpose(
        attention[: 3 * WIDTH].reshape(3, WIDTH, HALF), (1, 0, 2)
    ).astype(F32)
    output_grad = side_by_side(attention[3 * WIDTH :], 2).astype(F32)
    expand_grad = side_by_side(total[1], 4).astype(F32)
    reduce_grad = side_by_side(total[2], 2).astype(F32)
    project_bias_grad = lax.dynamic_slice(small_total, (6, t * HALF), (2, HALF))
    expand_bias_grad = lax.dynamic_slice(small_total, (8 + 2 * t, 0), (2, WIDTH)).reshape(-1)
    return (
        own_tokens(block_out),
        own_tokens(input_grad),
        small_total[0],
        small_total[1],
        project_grad,
        project_bias_grad,
        output_grad,
        small_total[4],
        small_total[2],
        small_total[3],
        expand_grad,
        expand_bias_grad,
        reduce_grad,
        small_total[5],
    )


def solution(mesh):
    in_specs = (
        P(("dp", "tensor"), None, None),
        P("dp"),
        P(),
        P(),
        P(None, None, "tensor"),
        P(None, "tensor"),
        P("tensor", None),
        P(),
        P(),
        P(),
        P(None, "tensor"),
        P("tensor"),
        P("tensor", None),
        P(),
        P(("dp", "tensor"), None, None),
    )
    out_specs = (
        P(("dp", "tensor"), None, None),
        P(("dp", "tensor"), None, None),
        P(),
        P(),
        P(None, None, "tensor"),
        P(None, "tensor"),
        P("tensor", None),
        P(),
        P(),
        P(),
        P(None, "tensor"),
        P("tensor"),
        P("tensor", None),
        P(),
    )
    return jax.shard_map(shards, mesh=mesh, in_specs=in_specs, out_specs=out_specs, check_vma=False)
```

```python
import functools

import jax
import jax.numpy as jnp
from jax import lax
from jax.experimental import pallas as pl
from jax.experimental.pallas import tpu as pltpu
from jax.sharding import PartitionSpec as P

HD = 64
EPSILON = 1e-06
TOKENS = 197
ROWS = 208
BOTH = 2 * ROWS
WIDTH = 768
HALF = 384
PAIRS = 6
BLOCK = 48
THIRD = 16
MESH = pl.DeviceIdType.MESH
F32 = jnp.float32
BF16 = jnp.bfloat16
ANY = pl.BlockSpec(memory_space=pl.ANY)
VMEM = pl.BlockSpec(memory_space=pltpu.VMEM)
SMEM = pl.BlockSpec(memory_space=pltpu.SMEM)


class Place:
    def __init__(self):
        dp, t = lax.axis_index("dp"), lax.axis_index("tensor")
        self.dp, self.t = dp, t
        c, y = lax.rem(dp, 2), lax.rem(lax.div(dp, 2), 4)
        zl, x = lax.rem(lax.div(dp, 8), 2), lax.div(dp, 16)
        z = t * 2 + zl
        self.c, self.other_c = c, 1 - c
        self.zl, self.other_zl = zl, 1 - zl
        kinds = {"own": 0, "up": 1, "far": 2, "down": 3}
        self.x = {kind: lax.rem(x + step, 4) for kind, step in kinds.items()}
        self.y = {kind: lax.rem(y + step, 4) for kind, step in kinds.items()}
        depth = {kind: lax.rem(z + step, 4) for kind, step in kinds.items()}
        self.z_low = {kind: lax.rem(d, 2) for kind, d in depth.items()}
        self.side = {kind: lax.rem(lax.div(d, 2) + t, 2) for kind, d in depth.items()}

        def at(x, y, z, c):
            return (((x * 2 + lax.rem(z, 2)) * 4 + y) * 2 + c, lax.div(z, 2))

        self.to = {
            "x": tuple(at(self.x[kind], y, z, c) for kind in ("up", "down", "far")),
            "y": tuple(at(x, self.y[kind], z, c) for kind in ("up", "down", "far")),
            "z": tuple(at(x, y, depth[kind], c) for kind in ("up", "down", "far")),
        }
        self.to_core = at(x, y, z, 1 - c)
        self.to_low = at(x, y, t * 2 + 1 - zl, c)
        self.to_half = at(x, y, 3 - z, c)
        self.butterfly = [
            self.to_core,
            at(x + 1 - 2 * lax.rem(x, 2), y, z, c),
            at(3 - x, y, z, c),
            at(x, y + 1 - 2 * lax.rem(y, 2), z, c),
            at(x, 3 - y, z, c),
            at(x, y, z + 1 - 2 * lax.rem(z, 2), c),
            at(x, y, 3 - z, c),
        ]

    def greet(self):
        devices = [self.to_core, *self.to["x"], *self.to["y"], *self.to["z"]]
        barrier = pltpu.get_barrier_semaphore()
        for device in devices:
            pl.semaphore_signal(barrier, inc=1, device_id=device, device_id_type=MESH)
        pl.semaphore_wait(barrier, len(devices))


class Post:
    def __init__(self, send_sems, recv_sems):
        self.send_sems, self.recv_sems, self.copies = send_sems, recv_sems, []

    def describe(self, src, dst, device, k):
        return pltpu.make_async_remote_copy(
            src_ref=src,
            dst_ref=dst,
            send_sem=self.send_sems.at[k],
            recv_sem=self.recv_sems.at[k],
            device_id=device,
            device_id_type=MESH,
        )

    def send(self, src, dst, device):
        copy = self.describe(src, dst, device, len(self.copies))
        copy.start()
        self.copies.append(copy)
        return copy

    def drain(self):
        for copy in self.copies:
            copy.wait_send()


ALL = slice(None)
ATTENTION, FEED = 0, 1


def gather_steps(me, post, out, group):
    kinds = 0 if group == ATTENTION else pl.ds(1, 2)
    x, y, zl, zo, c = me.x, me.y, me.zl, me.other_zl, me.c
    (xr, xl, xf), (yr, yl, yf) = me.to["x"], me.to["y"]

    def view(third, at_x, at_zl, at_y):
        return out.at[kinds, at_x, at_zl, at_y, c, pl.ds(third * THIRD, THIRD)]

    def put(device, *spot):
        ref = view(*spot)
        return post.send(ref, ref, device)

    def share(*spot):
        cores.append(put(me.to_core, *spot))

    def wait(*copies):
        for copy in copies:
            copy.wait_recv()

    cores = []
    X, Y = x["own"], y["own"]
    a1 = put(me.to_low, 0, X, zl, Y)
    b1 = [put(device, 1, X, zl, Y) for device in (xr, xl, xf)]
    d1 = [put(device, 2, X, zl, Y) for device in (yr, yl, yf)]
    yield
    wait(a1)
    a2 = [put(device, 0, X, ALL, Y) for device in (yr, yl, yf)]
    wait(*d1)
    d2 = [put(device, 2, X, zl, ALL) for device in (xr, xl, xf)]
    wait(*b1)
    b2 = put(me.to_low, 1, ALL, zl, Y)
    d3 = [put(me.to_low, 2, X, zl, ALL)]
    share(2, X, zl, ALL)
    yield
    wait(*a2)
    a3r, a3l = put(xr, 0, X, ALL, ALL), put(xl, 0, X, ALL, ALL)
    wait(b2)
    b3r, b3l = put(yr, 1, ALL, ALL, Y), put(yl, 1, ALL, ALL, Y)
    wait(*d2)
    for kind in ("down", "up", "far"):
        d3.append(put(me.to_low, 2, x[kind], zl, ALL))
    share(0, X, ALL, ALL)
    share(1, ALL, ALL, Y)
    for kind in ("down", "up", "far"):
        share(2, x[kind], zl, ALL)
    yield
    wait(a3r)
    a3fr = put(xr, 0, x["down"], 0, ALL)
    wait(a3l)
    a3fl = put(xl, 0, x["up"], 1, ALL)
    wait(b3r)
    b3fr = put(yr, 1, ALL, 0, y["down"])
    wait(b3l)
    b3fl = put(yl, 1, ALL, 1, y["up"])
    share(0, x["down"], ALL, ALL)
    share(0, x["up"], ALL, ALL)
    share(1, ALL, ALL, y["down"])
    share(1, ALL, ALL, y["up"])
    for copy, kind in zip(d3[:2], ("own", "down")):
        wait(copy)
        share(2, x[kind], zo, ALL)
    yield
    for copy, kind in zip(d3[2:], ("up", "far")):
        wait(copy)
        share(2, x[kind], zo, ALL)
    wait(a3fr, a3fl)
    share(0, x["far"], ALL, ALL)
    wait(b3fr, b3fl)
    share(1, ALL, ALL, y["far"])
    yield
    wait(*cores)


GATHER_COPIES = 7 + 8 + 4 + 3 + 4 + 16


def other_weights_start(me, post, project, output, expand, reduce, weights):
    place = (me.x["own"], me.other_zl, me.y["own"], me.c)
    slots = [weights.at[(1, part, *place)] for part in range(3)]
    first = post.describe(slots[0], slots[0], me.to_half, 0)
    post.copies.append(first)
    column = [pl.multiple_of(k * HALF, HALF) for k in (me.x["own"], me.half_x, me.other_zl)]

    @pl.when(me.x["own"] < 3)
    def _():
        post.describe(project.at[place], slots[0], me.to_half, 0).start()

    @pl.when(me.x["own"] >= 3)
    def _():
        src = output.at[me.y["own"], me.c, :, pl.ds(column[2], HALF)]
        post.describe(src, slots[0], me.to_half, 0).start()

    src = expand.at[me.other_zl, me.y["own"], me.c, :, pl.ds(column[0], HALF)]
    second = post.send(src, slots[1], me.to_half)
    src = reduce.at[me.odd_x, me.other_zl, me.y["own"], me.c, :, pl.ds(column[1], HALF)]
    third = post.send(src, slots[2], me.to_half)
    return first, second, third


AXES = ("xyz", "yzx", "zxy")


def grad_view(grads, me, group, third, stage, half, kind):
    order = AXES[third]
    spot = {"o": ALL, "x": ALL, "zl": ALL, "y": ALL}
    for n, axis in enumerate(order[: stage + 1]):
        at = kind if n == stage else "own"
        if axis == "z":
            spot["o"], spot["zl"] = me.side[at], me.z_low[at]
        else:
            spot[axis] = getattr(me, axis)[at]
    if half is None:
        part = 0 if group == ATTENTION else pl.ds(1, 2)
    elif group == FEED:
        part = 1 + half
    else:
        part = 0
        left = order[stage + 1 :]
        if "z" in left:
            spot["o"] = half
        else:
            spot[left[0]] = pl.ds(2 * half, 2)
    rows = pl.ds(third * THIRD, THIRD)
    return grads.at[spot["o"], part, spot["x"], spot["zl"], spot["y"], me.c, rows]


HELD = (
    (((6, 2, 4), (6, 4, 2), (6, 2, 4)), ((3, 2, 2), (3, 4), (3, 4)), ((3,), (3,), (3,))),
    (
        ((6, 2, 2, 4), (6, 2, 4, 2), (6, 4, 4)),
        ((3, 2, 2, 2), (3, 2, 4), (3, 2, 4)),
        ((3, 2), (3, 2), (3, 2)),
    ),
)


def add_into(ref, bufs):
    total = ref[...].astype(F32)
    for buf in bufs:
        total = total + buf[...].astype(F32)
    ref[...] = total.astype(BF16)


class Direct:
    def __init__(self, me, post, grads, bufs, group, third, stage):
        self.view = lambda kind: grad_view(grads, me, group, third, stage, None, kind)
        self.bufs = [bufs.at[i] for i in range(3)]
        self.copies = [
            post.send(self.view(kind), buf, device)
            for kind, buf, device in zip(
                ("up", "down", "far"), self.bufs, me.to[AXES[third][stage]]
            )
        ]

    def finish(self):
        for copy in self.copies:
            copy.wait_recv()
        add_into(self.view("own"), self.bufs)


class Ring:
    def __init__(self, me, post, grads, bufs, group, third, stage):
        self.me, self.post, self.grads = me, post, grads
        self.key = (group, third, stage)
        self.right, self.left, _ = me.to[AXES[third][stage]]
        self.relay_l, self.relay_r, self.left_a, self.left_b, self.right_a, self.right_b = (
            bufs.at[i] for i in range(6)
        )

    def view(self, half, kind):
        group, third, stage = self.key
        return grad_view(self.grads, self.me, group, third, stage, half, kind)

    def add(self, half, kind, bufs):
        add_into(self.view(half, kind), bufs)

    def start(self):
        self.far_r = self.post.send(self.view(0, "far"), self.relay_l, self.right)
        self.far_l = self.post.send(self.view(1, "far"), self.relay_r, self.left)
        self.near_r = self.post.send(self.view(1, "up"), self.left_b, self.right)
        self.near_l = self.post.send(self.view(0, "down"), self.right_a, self.left)

    def relay(self):
        self.far_r.wait_recv()
        self.add(0, "up", [self.relay_l])
        self.last_r = self.post.send(self.view(0, "up"), self.left_a, self.right)
        self.far_l.wait_recv()
        self.add(1, "down", [self.relay_r])
        self.last_l = self.post.send(self.view(1, "down"), self.right_b, self.left)

    def finish(self):
        self.near_r.wait_recv()
        self.near_l.wait_recv()
        self.last_r.wait_recv()
        self.add(0, "own", [self.left_a, self.right_a])
        self.last_l.wait_recv()
        self.add(1, "own", [self.left_b, self.right_b])


def sum_steps(me, post, grads, theirs, bufs, out, own_sem, group):
    kinds = 0 if group == ATTENTION else pl.ds(1, 2)
    core = []
    if group == ATTENTION:
        for at in (3, 0, 1, 2):
            src = grads.at[:, 0, at, :, :, me.other_c]
            core.append(post.send(src, theirs.at[:, 0, at], me.to_core))
            yield
        for at, copy in zip((3, 0, 1, 2), core):
            copy.wait_recv()

            def step(o, carry, at=at):
                add_into(grads.at[o, 0, at, :, :, me.c], [theirs.at[o, 0, at]])
                return carry

            lax.fori_loop(0, 2, step, 0)
    else:
        for o in range(2):
            src = grads.at[o, kinds, :, :, :, me.other_c]
            core.append(post.send(src, theirs.at[o, kinds], me.to_core))
            yield
        for o in range(2):
            core[o].wait_recv()

            def step(k, carry, o=o):
                part, at = 1 + lax.div(k, 4), lax.rem(k, 4)
                add_into(grads.at[o, part, at, :, :, me.c], [theirs.at[o, part, at]])
                return carry

            lax.fori_loop(0, 8, step, 0)
            if o == 0:
                yield
    rings = [Ring(me, post, grads, bufs[0][third], group, third, 0) for third in range(3)]
    for ring in rings:
        ring.start()
    yield
    for ring in rings:
        ring.relay()
    yield
    for stage in range(1, 3):
        lines = []
        for third, ring in enumerate(rings):
            ring.finish()
            lines.append(Direct(me, post, grads, bufs[stage][third], group, third, stage))
        rings = lines
        yield
    for ring in rings:
        ring.finish()
    X, Y = me.x["own"], me.y["own"]
    local = pltpu.make_async_copy(
        grads.at[0, kinds, X, me.zl, Y, me.c], out.at[kinds, X, me.zl, Y, me.c], own_sem
    )
    local.start()
    local.wait()
    yield from gather_steps(me, post, out, group)


def small_steps(me, post, acc, arrived):
    for k, partner in enumerate(me.butterfly):
        copy = post.send(acc.at[k], arrived.at[k], partner)
        yield
        copy.wait_recv()
        acc[k + 1] = acc[k] + arrived[k]


COPIES = 4 + 4 * GATHER_COPIES + 6 + 2 * 3 * (6 + 3 + 3) + 7


def dot(a, b, dims=((1,), (0,))):
    return lax.dot_general(a, b, (dims, ((), ())), preferred_element_type=F32)


NT = ((1,), (1,))
TN = ((0,), (0,))


def phi_terms(h):
    v = h * 0.7071067811865476
    v = jnp.clip(v, -3.7439211627767994, 3.7439211627767994)
    s = v * v
    top = 0.00022905065861350646
    for k in (0.0034082910107109506, 0.050955695062380861, 0.18520832239976145, 1.128379143519084):
        top = top * s + k
    low = -1.1791602954361697e-7
    for k in (
        0.000023547966471313185,
        0.0010179625278914885,
        0.014070470171167667,
        0.11098505178285362,
        0.49746925110067538,
        1.0,
    ):
        low = low * s + k
    big = 0.5 + 0.5 * (v * top / low)
    small = jnp.exp(h * h * -0.5) * 0.3989422804014327
    return big, big + h * small


def norm_stats(v):
    center = jnp.mean(v, axis=-1, keepdims=True)
    centered = v - center
    spread = jnp.mean(centered * centered, axis=-1, keepdims=True)
    scale = lax.rsqrt(spread + EPSILON)
    return centered * scale, scale


def row_loop(step, rows=16, start=0, stop=BOTH):
    def body(k, carry):
        step(pl.ds(pl.multiple_of(k * rows, rows), rows))
        return carry

    lax.fori_loop(start // rows, stop // rows, body, 0)


def poke(*steps):
    for step in steps:
        next(step, None)


def finish(*steps):
    for step in steps:
        for _ in step:
            pass


def layer_kernel(
    counts,
    x_in,
    cot_in,
    vectors,
    small_mine,
    project,
    output,
    expand,
    reduce,
    block_out,
    input_grad,
    total_out,
    small_out,
    weights,
    grads,
    theirs,
    *rest,
):
    bufs = [[rest[9 * g + 3 * s : 9 * g + 3 * s + 3] for s in range(3)] for g in range(2)]
    (
        small_other,
        acc,
        arrived,
        block_low,
        resid,
        grad_resid,
        go,
        normed,
        normed_two,
        qkv,
        mixed,
        grad_mixed,
        probs,
        hidden,
        active,
        grad_hidden,
        branch,
        dnorm,
        grad_attended,
        grad_qkv,
        sums,
        w_sems,
        own_sems,
        send_sems,
        recv_sems,
    ) = rest[18:]
    me = Place()
    me.half_x, me.odd_x = lax.div(me.x["own"], 2), lax.rem(me.x["own"], 2)
    t = me.t
    first = t == 0
    loads = []

    def load(src, dst):
        copy = pltpu.make_async_copy(src, dst, w_sems.at[len(loads)])
        copy.start()
        loads.append(copy)

    cols = [pl.ds(k * HALF, HALF) for k in range(4)]
    for j in range(3):
        load(project.at[j], weights.at[0, 0, j])
    for k in range(2):
        load(output.at[:, :, :, cols[k]], weights.at[0, 0, 3, k])
    for k in range(4):
        load(expand.at[:, :, :, :, cols[k]], weights.at[0, 1, k])
    for k in range(4):
        load(reduce.at[k % 2, :, :, :, :, cols[k // 2]], weights.at[0, 2, k])

    me.greet()
    post = Post(send_sems, recv_sems)
    pieces = other_weights_start(me, post, project, output, expand, reduce, weights)
    small_copy = post.send(small_mine, small_other, me.to_half)

    def weight_steps(group):
        yield
        for piece in pieces[:1] if group == ATTENTION else pieces[1:]:
            piece.wait_recv()
        yield from gather_steps(me, post, weights.at[1], group)

    wa, wf = weight_steps(ATTENTION), weight_steps(FEED)
    poke(wa, wf)

    live = counts[0] - 2 * t
    keep = [jnp.where(live > i, 1.0, 0.0) for i in range(2)]
    first_gain, first_shift = vectors[0:1], vectors[1:2]
    second_gain, second_shift = vectors[2:3], vectors[3:4]
    output_bias, reduce_bias = vectors[4:5], vectors[5:6]
    sums[...] = jnp.zeros_like(sums)

    def gather_sum(row, value):
        sums[pl.ds(row * 8, 8)] += value.reshape(-1, 8, WIDTH).sum(axis=0)

    def first_norm(rows):
        v = x_in[rows].astype(F32)
        n, _ = norm_stats(v)
        normed[rows] = (n * first_gain + first_shift).astype(BF16)

    row_loop(first_norm, 16, 0, ROWS)
    poke(wa)
    row_loop(first_norm, 16, ROWS, BOTH)
    poke(wa)
    for i in range(2):
        own = pl.ds(i * ROWS, ROWS)
        go[own] = (cot_in[own].astype(F32) * keep[i]).astype(BF16)

    lane = lax.broadcasted_iota(jnp.int32, (ROWS, 128), 1)
    first_head = lane < HD

    def split(pair):
        zero = jnp.zeros_like(pair)
        return jnp.concatenate(
            [jnp.where(first_head, pair, zero), jnp.where(first_head, zero, pair)], axis=0
        )

    def joined(both):
        return jnp.where(first_head, both[:ROWS], both[ROWS:])

    def image_rows(i):
        return pl.ds(pl.multiple_of(i * ROWS, 16), ROWS)

    def slab(o, part, at):
        return weights[o, part, at].reshape(WIDTH, HALF)

    def beside(*blocks):
        return jnp.concatenate(blocks, axis=1)

    key_dead = lax.broadcasted_iota(jnp.int32, (2 * ROWS, ROWS), 1) >= TOKENS

    def attend(k, carry):
        p, rows = lax.div(k, 2), image_rows(lax.rem(k, 2))
        queries = split(qkv[0, p, rows] * jnp.asarray(HD**-0.5, BF16))
        scores = dot(queries, qkv[1, p, rows], NT)
        scores = jnp.where(key_dead, -1e30, scores)
        raised = jnp.exp(scores - jnp.max(scores, axis=-1, keepdims=True))
        soft = (raised / jnp.sum(raised, axis=-1, keepdims=True)).astype(BF16)
        probs[k] = soft
        mixed[p, rows] = joined(dot(soft, qkv[2, p, rows])).astype(BF16)
        return carry

    for o in range(2):
        if o == 0:
            for copy in loads[:3]:
                copy.wait()
        else:
            finish(wa)
            small_copy.wait_recv()
        small = small_mine if o == 0 else small_other
        for j in range(3):
            result = (dot(normed[...], slab(o, 0, j)) + small[j : j + 1]).astype(BF16)
            for p in range(3):
                qkv[j, 3 * o + p] = result[:, 128 * p : 128 * (p + 1)]
            poke(wa, *([wf] if j == 2 or o == 1 else []))
        for k in range(0, 6, 2):
            lax.fori_loop(6 * o + k, 6 * o + k + 2, attend, 0)
            poke(wa, wf)

    def all_pairs(ref):
        return jnp.concatenate([ref[p] for p in range(PAIRS)], axis=1)

    for copy in loads[3:5]:
        copy.wait()

    def output_matrix():
        return jnp.concatenate(
            [
                beside(*(weights[o, 0, 3, k].reshape(HALF, HALF) for k in range(2)))
                for o in range(2)
            ],
            axis=0,
        )

    resid[...] = dot(all_pairs(mixed), output_matrix())
    poke(wf)

    def second_norm(rows):
        v = resid[rows] + x_in[rows].astype(F32) + output_bias
        resid[rows] = v
        n, _ = norm_stats(v)
        normed_two[rows] = (n * second_gain + second_shift).astype(BF16)

    row_loop(second_norm)
    poke(wf)

    for copy in loads[5:]:
        copy.wait()
    branch[...] = jnp.zeros_like(branch)
    dnorm[...] = jnp.zeros_like(dnorm)

    def feed(o, jj):
        small = small_mine if o == 0 else small_other
        bias = beside(small[pl.ds(3 + 2 * jj, 1)], small[pl.ds(4 + 2 * jj, 1)])
        w_expand = beside(slab(o, 1, 2 * jj), slab(o, 1, 2 * jj + 1))
        hidden[...] = dot(normed_two[...], w_expand) + bias

        def gelu(rows):
            h = hidden[rows]
            big, slope_rows = phi_terms(h)
            active[rows] = (h * big).astype(BF16)
            hidden[rows] = slope_rows

        row_loop(gelu)
        w_reduce = beside(slab(o, 2, jj), slab(o, 2, 2 + jj))
        branch[...] += dot(active[...], w_reduce)
        gh = (dot(go[...], w_reduce, NT) * hidden[...]).astype(BF16)
        grad_hidden[...] = gh
        row = (8 + 2 * o + jj) * 8
        sums[pl.ds(row, 8)] = gh.astype(F32).reshape(-1, 8, WIDTH).sum(axis=0)
        dnorm[...] += dot(grad_hidden[...], w_expand, NT)
        grad = dot(normed_two[...], grad_hidden[...], TN).astype(BF16)
        grads[o, 1, 2 * jj] = grad[:, :HALF].reshape(2, 4, 2, BLOCK, HALF)
        grads[o, 1, 2 * jj + 1] = grad[:, HALF:].reshape(2, 4, 2, BLOCK, HALF)
        grad = dot(active[...], go[...], TN).astype(BF16)
        grads[o, 2, jj] = grad[:, :HALF].reshape(2, 4, 2, BLOCK, HALF)
        grads[o, 2, 2 + jj] = grad[:, HALF:].reshape(2, 4, 2, BLOCK, HALF)

    sf = sum_steps(me, post, grads, theirs, bufs[1], total_out, own_sems.at[0], FEED)
    for jj in range(2):
        feed(0, jj)
        poke(wf)
    finish(wf)
    poke(sf)
    for jj in range(2):
        feed(1, jj)
    poke(sf)

    for i in range(2):
        own = pl.ds(i * ROWS, ROWS)
        block_low[own] = ((resid[own] + branch[own] + reduce_bias) * keep[i]).astype(BF16)
    block_store = pltpu.make_async_copy(block_low, block_out, own_sems.at[2])
    block_store.start()

    def norm_back(n, scale, grad, gain):
        e = grad * gain
        return scale * (
            e - jnp.mean(e, axis=-1, keepdims=True) - n * jnp.mean(e * n, axis=-1, keepdims=True)
        )

    def second_back(rows):
        n, scale = norm_stats(resid[rows])
        grad = dnorm[rows]
        total = go[rows].astype(F32)
        gather_sum(5, total)
        total = total + norm_back(n, scale, grad, second_gain)
        grad_resid[rows] = total
        low = total.astype(BF16)
        grad_attended[rows] = low
        gather_sum(2, grad * n)
        gather_sum(3, grad)
        gather_sum(4, low.astype(F32))

    row_loop(second_back)
    poke(sf)

    grad = dot(all_pairs(mixed), grad_attended[...], TN).astype(BF16)
    for o in range(2):
        for k in range(2):
            grads[o, 0, 3, k] = grad[
                o * HALF : (o + 1) * HALF, k * HALF : (k + 1) * HALF
            ].reshape(4, 2, BLOCK, HALF)
    sa = sum_steps(me, post, grads, theirs, bufs[0], total_out, own_sems.at[1], ATTENTION)
    poke(sa, sf)
    result = dot(grad_attended[...], output_matrix(), NT).astype(BF16)
    for p in range(PAIRS):
        grad_mixed[p] = result[:, 128 * p : 128 * (p + 1)]

    def attend_back(k, carry):
        p, rows = lax.div(k, 2), image_rows(lax.rem(k, 2))
        grad_out = split(grad_mixed[p, rows])
        soft_low = probs[k]
        soft = soft_low.astype(F32)
        grad_soft = dot(grad_out, qkv[2, p, rows], NT)
        inner = jnp.sum(soft * grad_soft, axis=-1, keepdims=True)
        grad_scores = (soft * (grad_soft - inner)).astype(BF16)
        scale = jnp.asarray(HD**-0.5, BF16)
        queries = split(qkv[0, p, rows] * scale)
        grad_qkv[0, p, rows] = joined(dot(grad_scores, qkv[1, p, rows] * scale)).astype(BF16)
        grad_qkv[1, p, rows] = dot(grad_scores, queries, TN).astype(BF16)
        grad_qkv[2, p, rows] = dot(soft_low, grad_out, TN).astype(BF16)
        return carry

    for k in range(0, 12, 6):
        lax.fori_loop(k, k + 6, attend_back, 0)
        poke(sf)

    for j in range(3):
        grad = dot(normed[...], all_pairs(grad_qkv.at[j]), TN).astype(BF16)
        for o in range(2):
            grads[o, 0, j] = grad[:, o * HALF : (o + 1) * HALF].reshape(2, 4, 2, BLOCK, HALF)
        poke(sa)
    poke(sf)
    for j in range(3):
        given = all_pairs(grad_qkv.at[j])
        back = dot(given, beside(slab(0, 0, j), slab(1, 0, j)), NT)
        if j == 0:
            dnorm[...] = back
        else:
            dnorm[...] += back
        if j != 1:
            row = 48 if j == 0 else 56
            sums[row : row + 8] = given.astype(F32).reshape(-1, 8, WIDTH).sum(axis=0)
        poke(sa, sf)

    def first_back(rows):
        n, scale = norm_stats(x_in[rows].astype(F32))
        grad = dnorm[rows]
        grad_resid[rows] = grad_resid[rows] + norm_back(n, scale, grad, first_gain)
        gather_sum(0, grad * n)
        gather_sum(1, grad)

    row_loop(first_back, 16, 0, ROWS)
    poke(sa, sf)
    row_loop(first_back, 16, ROWS, BOTH)
    input_store = pltpu.make_async_copy(grad_resid, input_grad, own_sems.at[3])
    input_store.start()

    totals = [jnp.sum(sums[8 * k : 8 * (k + 1)], axis=0, keepdims=True) for k in range(12)]

    def swapped(row):
        return jnp.where(first, row, jnp.concatenate([row[:, HALF:], row[:, :HALF]], axis=1))

    rows = totals[:6] + [swapped(totals[6]), swapped(totals[7])]
    for k in range(4):
        rows.append(jnp.where(first, totals[8 + k], totals[8 + (k + 2) % 4]))
    for k in range(12):
        acc[0, k : k + 1] = rows[k]
    acc[0, 12:16] = jnp.zeros((4, WIDTH), F32)
    sm = small_steps(me, post, acc, arrived)
    for _ in range(16):
        poke(sa, sm, sf)
    finish(sf, sm, sa)
    small_out[...] = acc[7]
    post.drain()
    block_store.wait()
    input_store.wait()


def layer(counts, x, cot, vectors, small, project, output, expand, reduce):
    def buf(*shape, dtype=BF16):
        return pltpu.VMEM(shape, dtype)

    ring_bufs = [
        buf(*HELD[group][stage][third], THIRD, HALF)
        for group in range(2)
        for stage in range(3)
        for third in range(3)
    ]
    blocks = (3, 4, 2, 4, 2, BLOCK, HALF)
    return pl.pallas_call(
        layer_kernel,
        out_shape=(
            jax.ShapeDtypeStruct((BOTH, WIDTH), BF16),
            jax.ShapeDtypeStruct((BOTH, WIDTH), F32),
            jax.ShapeDtypeStruct(blocks, BF16),
            jax.ShapeDtypeStruct((16, WIDTH), F32),
        ),
        in_specs=[SMEM] + [VMEM] * 4 + [ANY] * 4,
        out_specs=(ANY, ANY, ANY, VMEM),
        scratch_shapes=[
            buf(2, *blocks),
            buf(2, *blocks),
            buf(2, 3, 4, 2, 4, BLOCK, HALF),
            *ring_bufs,
            buf(*small.shape, dtype=F32),
            buf(8, 16, WIDTH, dtype=F32),
            buf(7, 16, WIDTH, dtype=F32),
            buf(BOTH, WIDTH),
            buf(BOTH, WIDTH, dtype=F32),
            buf(BOTH, WIDTH, dtype=F32),
            buf(BOTH, WIDTH),
            buf(BOTH, WIDTH),
            buf(BOTH, WIDTH),
            buf(3, PAIRS, BOTH, 128),
            buf(PAIRS, BOTH, 128),
            buf(PAIRS, BOTH, 128),
            buf(2 * PAIRS, 2 * ROWS, ROWS),
            buf(BOTH, WIDTH, dtype=F32),
            buf(BOTH, WIDTH),
            buf(BOTH, WIDTH),
            buf(BOTH, WIDTH, dtype=F32),
            buf(BOTH, WIDTH, dtype=F32),
            buf(BOTH, WIDTH),
            buf(3, PAIRS, BOTH, 128),
            buf(12 * 8, WIDTH, dtype=F32),
            pltpu.SemaphoreType.DMA((13,)),
            pltpu.SemaphoreType.DMA((4,)),
            pltpu.SemaphoreType.DMA((COPIES,)),
            pltpu.SemaphoreType.DMA((COPIES,)),
        ],
        compiler_params=pltpu.CompilerParams(
            collective_id=0, has_side_effects=True, vmem_limit_bytes=63 << 20
        ),
        name="layer",
    )(counts, x, cot, vectors, small, project, output, expand, reduce)


def shards(
    inputs,
    image_counts,
    first_gain,
    first_shift,
    project_weight,
    project_bias,
    output_weight,
    output_bias,
    second_gain,
    second_shift,
    expand_weight,
    expand_bias,
    reduce_weight,
    reduce_bias,
    out_cotangent,
):
    small = jnp.concatenate(
        [
            project_bias[0:1],
            jnp.zeros((1, HALF), F32),
            project_bias[1:2],
            expand_bias.reshape(4, HALF),
            jnp.zeros((1, HALF), F32),
        ]
    )
    vectors = jnp.stack(
        [first_gain, first_shift, second_gain, second_shift, output_bias, reduce_bias, first_gain, first_gain]
    )

    def padded(array):
        return jnp.pad(array, ((0, 0), (0, ROWS - TOKENS), (0, 0))).reshape(BOTH, WIDTH)

    block_out, input_grad, total, small_total = layer(
        image_counts,
        padded(inputs),
        padded(out_cotangent),
        vectors,
        small,
        jnp.transpose(project_weight, (1, 0, 2)).reshape(3, 2, 4, 2, BLOCK, HALF),
        output_weight.reshape(4, 2, BLOCK, WIDTH),
        expand_weight.reshape(2, 4, 2, BLOCK, 4 * HALF),
        reduce_weight.reshape(2, 2, 4, 2, BLOCK, WIDTH),
    )
    total = total.reshape(3, 4 * WIDTH, HALF)
    t = lax.axis_index("tensor")

    def own_tokens(array):
        return array.reshape(2, ROWS, WIDTH)[:, :TOKENS]

    def side_by_side(array, count):
        rows = array.shape[0] // count
        return jnp.transpose(array.reshape(count, rows, HALF), (1, 0, 2)).reshape(
            rows, count * HALF
        )

    attention = total[0]
    project_grad = jnp.transpose(
        attention[: 3 * WIDTH].reshape(3, WIDTH, HALF), (1, 0, 2)
    ).astype(F32)
    output_grad = side_by_side(attention[3 * WIDTH :], 2).astype(F32)
    expand_grad = side_by_side(total[1], 4).astype(F32)
    reduce_grad = side_by_side(total[2], 2).astype(F32)
    project_bias_grad = lax.dynamic_slice(small_total, (6, t * HALF), (2, HALF))
    expand_bias_grad = lax.dynamic_slice(small_total, (8 + 2 * t, 0), (2, WIDTH)).reshape(-1)
    return (
        own_tokens(block_out),
        own_tokens(input_grad),
        small_total[0],
        small_total[1],
        project_grad,
        project_bias_grad,
        output_grad,
        small_total[4],
        small_total[2],
        small_total[3],
        expand_grad,
        expand_bias_grad,
        reduce_grad,
        small_total[5],
    )


def solution(mesh):
    in_specs = (
        P(("dp", "tensor"), None, None),
        P("dp"),
        P(),
        P(),
        P(None, None, "tensor"),
        P(None, "tensor"),
        P("tensor", None),
        P(),
        P(),
        P(),
        P(None, "tensor"),
        P("tensor"),
        P("tensor", None),
        P(),
        P(("dp", "tensor"), None, None),
    )
    out_specs = (
        P(("dp", "tensor"), None, None),
        P(("dp", "tensor"), None, None),
        P(),
        P(),
        P(None, None, "tensor"),
        P(None, "tensor"),
        P("tensor", None),
        P(),
        P(),
        P(),
        P(None, "tensor"),
        P("tensor"),
        P("tensor", None),
        P(),
    )
    return jax.shard_map(shards, mesh=mesh, in_specs=in_specs, out_specs=out_specs, check_vma=False)
```

```python
import functools

import jax
import jax.numpy as jnp
from jax import lax
from jax.experimental import pallas as pl
from jax.experimental.pallas import tpu as pltpu
from jax.sharding import PartitionSpec as P

HD = 64
EPSILON = 1e-06
TOKENS = 197
ROWS = 208
BOTH = 2 * ROWS
WIDTH = 768
HALF = 384
PAIRS = 6
BLOCK = 48
THIRD = 16
MESH = pl.DeviceIdType.MESH
F32 = jnp.float32
BF16 = jnp.bfloat16
ANY = pl.BlockSpec(memory_space=pl.ANY)
VMEM = pl.BlockSpec(memory_space=pltpu.VMEM)
SMEM = pl.BlockSpec(memory_space=pltpu.SMEM)


class Place:
    def __init__(self):
        dp, t = lax.axis_index("dp"), lax.axis_index("tensor")
        self.dp, self.t = dp, t
        c, y = lax.rem(dp, 2), lax.rem(lax.div(dp, 2), 4)
        zl, x = lax.rem(lax.div(dp, 8), 2), lax.div(dp, 16)
        z = t * 2 + zl
        self.c, self.other_c = c, 1 - c
        self.zl, self.other_zl = zl, 1 - zl
        kinds = {"own": 0, "up": 1, "far": 2, "down": 3}
        self.x = {kind: lax.rem(x + step, 4) for kind, step in kinds.items()}
        self.y = {kind: lax.rem(y + step, 4) for kind, step in kinds.items()}
        depth = {kind: lax.rem(z + step, 4) for kind, step in kinds.items()}
        self.z_low = {kind: lax.rem(d, 2) for kind, d in depth.items()}
        self.side = {kind: lax.rem(lax.div(d, 2) + t, 2) for kind, d in depth.items()}

        def at(x, y, z, c):
            return (((x * 2 + lax.rem(z, 2)) * 4 + y) * 2 + c, lax.div(z, 2))

        self.to = {
            "x": tuple(at(self.x[kind], y, z, c) for kind in ("up", "down", "far")),
            "y": tuple(at(x, self.y[kind], z, c) for kind in ("up", "down", "far")),
            "z": tuple(at(x, y, depth[kind], c) for kind in ("up", "down", "far")),
        }
        self.to_core = at(x, y, z, 1 - c)
        self.to_low = at(x, y, t * 2 + 1 - zl, c)
        self.to_half = at(x, y, 3 - z, c)
        self.butterfly = [
            self.to_core,
            at(x + 1 - 2 * lax.rem(x, 2), y, z, c),
            at(3 - x, y, z, c),
            at(x, y + 1 - 2 * lax.rem(y, 2), z, c),
            at(x, 3 - y, z, c),
            at(x, y, z + 1 - 2 * lax.rem(z, 2), c),
            at(x, y, 3 - z, c),
        ]

    def greet(self):
        devices = [self.to_core, *self.to["x"], *self.to["y"], *self.to["z"]]
        barrier = pltpu.get_barrier_semaphore()
        for device in devices:
            pl.semaphore_signal(barrier, inc=1, device_id=device, device_id_type=MESH)
        pl.semaphore_wait(barrier, len(devices))


class Post:
    def __init__(self, send_sems, recv_sems):
        self.send_sems, self.recv_sems, self.copies = send_sems, recv_sems, []

    def describe(self, src, dst, device, k):
        return pltpu.make_async_remote_copy(
            src_ref=src,
            dst_ref=dst,
            send_sem=self.send_sems.at[k],
            recv_sem=self.recv_sems.at[k],
            device_id=device,
            device_id_type=MESH,
        )

    def send(self, src, dst, device):
        copy = self.describe(src, dst, device, len(self.copies))
        copy.start()
        self.copies.append(copy)
        return copy

    def drain(self):
        for copy in self.copies:
            copy.wait_send()


ALL = slice(None)
GROUPS = 3


def gather_steps(me, post, out, group):
    x, y, zl, zo, c = me.x, me.y, me.zl, me.other_zl, me.c
    (xr, xl, xf), (yr, yl, yf) = me.to["x"], me.to["y"]

    def view(third, at_x, at_zl, at_y):
        return out.at[group, at_x, at_zl, at_y, c, pl.ds(third * THIRD, THIRD)]

    def put(device, *spot):
        ref = view(*spot)
        return post.send(ref, ref, device)

    def share(*spot):
        cores.append(put(me.to_core, *spot))

    def wait(*copies):
        for copy in copies:
            copy.wait_recv()

    cores = []
    X, Y = x["own"], y["own"]
    a1 = put(me.to_low, 0, X, zl, Y)
    b1 = [put(device, 1, X, zl, Y) for device in (xf, xr, xl)]
    d1 = [put(device, 2, X, zl, Y) for device in (yf, yr, yl)]
    yield
    wait(a1)
    a2 = [put(device, 0, X, ALL, Y) for device in (yf, yr, yl)]
    wait(*d1)
    d2 = [put(device, 2, X, zl, ALL) for device in (xf, xr, xl)]
    wait(*b1)
    b2 = put(me.to_low, 1, ALL, zl, Y)
    yield
    wait(*a2)
    a3r, a3l = put(xr, 0, X, ALL, ALL), put(xl, 0, X, ALL, ALL)
    wait(b2)
    b3r, b3l = put(yr, 1, ALL, ALL, Y), put(yl, 1, ALL, ALL, Y)
    wait(*d2)
    d3 = put(me.to_low, 2, ALL, zl, ALL)
    share(0, X, ALL, ALL)
    share(1, ALL, ALL, Y)
    share(2, ALL, zl, ALL)
    yield
    wait(a3r)
    a3fr = put(xr, 0, x["down"], 0, ALL)
    wait(a3l)
    a3fl = put(xl, 0, x["up"], 1, ALL)
    wait(b3r)
    b3fr = put(yr, 1, ALL, 0, y["down"])
    wait(b3l)
    b3fl = put(yl, 1, ALL, 1, y["up"])
    share(0, x["down"], ALL, ALL)
    share(0, x["up"], ALL, ALL)
    share(1, ALL, ALL, y["down"])
    share(1, ALL, ALL, y["up"])
    yield
    wait(d3)
    share(2, ALL, zo, ALL)
    wait(a3fr, a3fl)
    share(0, x["far"], ALL, ALL)
    wait(b3fr, b3fl)
    share(1, ALL, ALL, y["far"])
    yield
    wait(*cores)


GATHER_COPIES = 7 + 7 + 5 + 4 + 10


def other_weights_start(me, post, project, output, expand, reduce, weights):
    x, row = me.x["own"], (me.other_zl, me.y["own"], me.c)
    slots = [weights.at[(1, group, x, *row)] for group in range(GROUPS)]
    pieces = []

    def columns(k):
        return pl.ds(pl.multiple_of(k * HALF, HALF), HALF)

    def either(group, split, low, high):
        piece = post.describe(slots[group], slots[group], me.to_half, group)
        post.copies.append(piece)
        pieces.append(piece)

        @pl.when(x < split)
        def _():
            post.describe(low(), slots[group], me.to_half, group).start()

        @pl.when(x >= split)
        def _():
            post.describe(high(), slots[group], me.to_half, group).start()

    either(
        0,
        3,
        lambda: project.at[(x, *row)],
        lambda: output.at[me.y["own"], me.c, :, columns(me.other_zl)],
    )
    for jj in range(2):
        either(
            1 + jj,
            2,
            lambda: expand.at[(*row, ALL, columns(2 * jj + x))],
            lambda: reduce.at[(jj, *row, ALL, columns(x - 2))],
        )
    return pieces


AXES = ("xyz", "yzx", "zxy")


def grad_view(grads, me, group, third, stage, half, kind):
    order = AXES[third]
    spot = {"o": ALL, "x": ALL, "zl": ALL, "y": ALL}
    for n, axis in enumerate(order[: stage + 1]):
        at = kind if n == stage else "own"
        if axis == "z":
            spot["o"], spot["zl"] = me.side[at], me.z_low[at]
        else:
            spot[axis] = getattr(me, axis)[at]
    if half is not None:
        left = order[stage + 1 :]
        if "z" in left:
            spot["o"] = half
        else:
            spot[left[0]] = pl.ds(2 * half, 2)
    rows = pl.ds(third * THIRD, THIRD)
    return grads.at[spot["o"], group, spot["x"], spot["zl"], spot["y"], me.c, rows]


HELD = (((6, 2, 4), (6, 4, 2), (6, 2, 4)), ((3, 2, 2), (3, 4), (3, 4)), ((3,), (3,), (3,)))


def add_into(ref, bufs):
    total = ref[...].astype(F32)
    for buf in bufs:
        total = total + buf[...].astype(F32)
    ref[...] = total.astype(BF16)


class Direct:
    def __init__(self, me, post, grads, bufs, group, third, stage):
        self.view = lambda kind: grad_view(grads, me, group, third, stage, None, kind)
        self.bufs = [bufs.at[i] for i in range(3)]
        self.copies = [
            post.send(self.view(kind), buf, device)
            for kind, buf, device in zip(
                ("up", "down", "far"), self.bufs, me.to[AXES[third][stage]]
            )
        ]

    def finish(self):
        for copy in self.copies:
            copy.wait_recv()
        add_into(self.view("own"), self.bufs)


class Ring:
    def __init__(self, me, post, grads, bufs, group, third, stage):
        self.me, self.post, self.grads = me, post, grads
        self.key = (group, third, stage)
        self.right, self.left, _ = me.to[AXES[third][stage]]
        self.relay_l, self.relay_r, self.left_a, self.left_b, self.right_a, self.right_b = (
            bufs.at[i] for i in range(6)
        )

    def view(self, half, kind):
        group, third, stage = self.key
        return grad_view(self.grads, self.me, group, third, stage, half, kind)

    def add(self, half, kind, bufs):
        add_into(self.view(half, kind), bufs)

    def start(self):
        self.far_r = self.post.send(self.view(0, "far"), self.relay_l, self.right)
        self.far_l = self.post.send(self.view(1, "far"), self.relay_r, self.left)
        self.near_r = self.post.send(self.view(1, "up"), self.left_b, self.right)
        self.near_l = self.post.send(self.view(0, "down"), self.right_a, self.left)

    def relay(self):
        self.far_r.wait_recv()
        self.add(0, "up", [self.relay_l])
        self.last_r = self.post.send(self.view(0, "up"), self.left_a, self.right)
        self.far_l.wait_recv()
        self.add(1, "down", [self.relay_r])
        self.last_l = self.post.send(self.view(1, "down"), self.right_b, self.left)

    def finish(self):
        self.near_r.wait_recv()
        self.near_l.wait_recv()
        self.last_r.wait_recv()
        self.add(0, "own", [self.left_a, self.right_a])
        self.last_l.wait_recv()
        self.add(1, "own", [self.left_b, self.right_b])


def sum_steps(me, post, grads, theirs, bufs, out, own_sem, group):
    core = []

    def add_slabs(count, spot):
        def step(k, carry):
            o, at = spot(k)
            add_into(grads.at[o, group, at, :, :, me.c], [theirs.at[o, group, at]])
            return carry

        lax.fori_loop(0, count, step, 0)

    if group == 0:
        for at in (3, 0, 1, 2):
            src = grads.at[:, 0, at, :, :, me.other_c]
            core.append(post.send(src, theirs.at[:, 0, at], me.to_core))
            yield
        for at, copy in zip((3, 0, 1, 2), core):
            copy.wait_recv()
            add_slabs(2, lambda k: (k, at))
    else:
        for o in range(2):
            src = grads.at[o, group, :, :, :, me.other_c]
            core.append(post.send(src, theirs.at[o, group], me.to_core))
            yield
        for o in range(2):
            core[o].wait_recv()
            add_slabs(4, lambda k: (o, k))
    rings = [Ring(me, post, grads, bufs[0][third], group, third, 0) for third in range(3)]
    for ring in rings:
        ring.start()
    yield
    for ring in rings:
        ring.relay()
    yield
    for stage in range(1, 3):
        lines = []
        for third, ring in enumerate(rings):
            ring.finish()
            lines.append(Direct(me, post, grads, bufs[stage][third], group, third, stage))
        rings = lines
        yield
    for ring in rings:
        ring.finish()
    X, Y = me.x["own"], me.y["own"]
    local = pltpu.make_async_copy(
        grads.at[0, group, X, me.zl, Y, me.c], out.at[group, X, me.zl, Y, me.c], own_sem
    )
    local.start()
    local.wait()
    yield from gather_steps(me, post, out, group)


def small_steps(me, post, acc, arrived):
    for k, partner in enumerate(me.butterfly):
        copy = post.send(acc.at[k], arrived.at[k], partner)
        yield
        copy.wait_recv()
        acc[k + 1] = acc[k] + arrived[k]


COPIES = 4 + 6 * GATHER_COPIES + 8 + 3 * 3 * (6 + 3 + 3) + 7


def dot(a, b, dims=((1,), (0,))):
    return lax.dot_general(a, b, (dims, ((), ())), preferred_element_type=F32)


NT = ((1,), (1,))
TN = ((0,), (0,))


def phi_terms(h):
    v = h * 0.7071067811865476
    v = jnp.clip(v, -3.7439211627767994, 3.7439211627767994)
    s = v * v
    top = 0.00022905065861350646
    for k in (0.0034082910107109506, 0.050955695062380861, 0.18520832239976145, 1.128379143519084):
        top = top * s + k
    low = -1.1791602954361697e-7
    for k in (
        0.000023547966471313185,
        0.0010179625278914885,
        0.014070470171167667,
        0.11098505178285362,
        0.49746925110067538,
        1.0,
    ):
        low = low * s + k
    big = 0.5 + 0.5 * (v * top / low)
    small = jnp.exp(h * h * -0.5) * 0.3989422804014327
    return big, big + h * small


def norm_stats(v):
    center = jnp.mean(v, axis=-1, keepdims=True)
    centered = v - center
    spread = jnp.mean(centered * centered, axis=-1, keepdims=True)
    scale = lax.rsqrt(spread + EPSILON)
    return centered * scale, scale


def row_loop(step, rows=16, start=0, stop=BOTH):
    def body(k, carry):
        step(pl.ds(pl.multiple_of(k * rows, rows), rows))
        return carry

    lax.fori_loop(start // rows, stop // rows, body, 0, unroll=True)


def poke(*steps):
    for step in steps:
        next(step, None)


def finish(*steps):
    for step in steps:
        for _ in step:
            pass


def layer_kernel(
    counts,
    x_in,
    cot_in,
    first_gain_in,
    first_shift_in,
    second_gain_in,
    second_shift_in,
    output_bias_in,
    reduce_bias_in,
    project_bias,
    expand_bias,
    project,
    output,
    expand,
    reduce,
    block_out,
    input_grad,
    total_out,
    small_out,
    weights,
    grads,
    theirs,
    *rest,
):
    bufs = [[rest[9 * g + 3 * s : 9 * g + 3 * s + 3] for s in range(3)] for g in range(GROUPS)]
    (
        small_mine,
        small_other,
        acc,
        arrived,
        block_low,
        stream,
        resid,
        grad_resid,
        go,
        normed,
        normed_two,
        qkv,
        mixed,
        probs,
        hidden,
        dnorm,
        grad_attended,
        sums,
        w_sems,
        own_sems,
        send_sems,
        recv_sems,
    ) = rest[27:]
    me = Place()
    t = me.t
    first = t == 0
    loads = []

    def load(src, dst):
        copy = pltpu.make_async_copy(src, dst, w_sems.at[len(loads)])
        copy.start()
        loads.append(copy)

    cols = [pl.ds(k * HALF, HALF) for k in range(4)]
    for j in range(3):
        load(project.at[j], weights.at[0, 0, j])
    for k in range(2):
        load(output.at[:, :, :, cols[k]], weights.at[0, 0, 3, k])
    for jj in range(2):
        for k in range(2):
            load(expand.at[:, :, :, :, cols[2 * jj + k]], weights.at[0, 1 + jj, k])
            load(reduce.at[jj, :, :, :, :, cols[k]], weights.at[0, 1 + jj, 2 + k])

    small_mine[...] = jnp.zeros_like(small_mine)
    small_mine[0:1] = project_bias[0:1]
    small_mine[2:3] = project_bias[1:2]
    for k in range(4):
        small_mine[3 + k : 4 + k] = expand_bias[k * HALF : (k + 1) * HALF].reshape(1, HALF)

    me.greet()
    post = Post(send_sems, recv_sems)
    pieces = other_weights_start(me, post, project, output, expand, reduce, weights)
    small_copy = post.send(small_mine, small_other, me.to_half)

    def weight_steps(group):
        yield
        pieces[group].wait_recv()
        yield from gather_steps(me, post, weights.at[1], group)

    wa, w0, w1 = (weight_steps(group) for group in range(GROUPS))
    poke(wa, w0, w1)

    live = counts[0] - 2 * t
    keep = [jnp.where(live > i, 1.0, 0.0) for i in range(2)]
    first_gain, first_shift, second_gain, second_shift, output_bias, reduce_bias = (
        ref[...].reshape(1, WIDTH)
        for ref in (
            first_gain_in,
            first_shift_in,
            second_gain_in,
            second_shift_in,
            output_bias_in,
            reduce_bias_in,
        )
    )
    sums[...] = jnp.zeros_like(sums)

    def gather_sum(row, value):
        sums[pl.ds(row * 8, 8)] += value.reshape(-1, 8, WIDTH).sum(axis=0)

    for i in range(2):
        for ref, given in ((stream, x_in), (go, cot_in)):

            def part(start, stop, ref=ref, given=given, i=i):
                rows = given[start:stop, i].astype(F32)
                return rows * keep[i] if ref is go else rows

            for start in range(0, 192, 16):
                at = i * ROWS + start
                ref[at : at + 16] = part(start, start + 16).astype(BF16)
            ends = jnp.concatenate([part(192, TOKENS), jnp.zeros((3, WIDTH), F32)], axis=0)
            ends = jnp.concatenate([ends, jnp.zeros((8, WIDTH), F32)], axis=0)
            ref[i * ROWS + 192 : (i + 1) * ROWS] = ends.astype(BF16)

    def first_norm(rows):
        v = stream[rows].astype(F32)
        n, _ = norm_stats(v)
        normed[rows] = (n * first_gain + first_shift).astype(BF16)

    row_loop(first_norm)
    poke(wa, w0, w1)

    lane = lax.broadcasted_iota(jnp.int32, (ROWS, 128), 1)
    first_head = lane < HD

    def split(pair):
        zero = jnp.zeros_like(pair)
        return jnp.concatenate(
            [jnp.where(first_head, pair, zero), jnp.where(first_head, zero, pair)], axis=0
        )

    def joined(both):
        return jnp.where(first_head, both[:ROWS], both[ROWS:])

    def image_rows(i):
        return pl.ds(pl.multiple_of(i * ROWS, 16), ROWS)

    def slab(o, part, at):
        return weights[o, part, at].reshape(WIDTH, HALF)

    def beside(*blocks):
        return jnp.concatenate(blocks, axis=1)

    key_dead = lax.broadcasted_iota(jnp.int32, (2 * ROWS, ROWS), 1) >= TOKENS

    def attend(k, carry):
        p, rows = lax.div(k, 2), image_rows(lax.rem(k, 2))
        queries = split(qkv[0, p, rows] * jnp.asarray(HD**-0.5, BF16))
        scores = dot(queries, qkv[1, p, rows], NT)
        scores = jnp.where(key_dead, -1e30, scores)
        raised = jnp.exp(scores - jnp.max(scores, axis=-1, keepdims=True))
        soft = (raised / jnp.sum(raised, axis=-1, keepdims=True)).astype(BF16)
        probs[k] = soft
        mixed[p, rows] = joined(dot(soft, qkv[2, p, rows])).astype(BF16)
        return carry

    for o in range(2):
        if o == 0:
            for copy in loads[:3]:
                copy.wait()
        else:
            finish(wa)
            small_copy.wait_recv()
            poke(w0, w1)
        small = small_mine if o == 0 else small_other
        for j in range(3):
            result = (dot(normed[...], slab(o, 0, j)) + small[j : j + 1]).astype(BF16)
            for p in range(3):
                qkv[j, 3 * o + p] = result[:, 128 * p : 128 * (p + 1)]
        for k in range(0, 6, 3):
            lax.fori_loop(6 * o + k, 6 * o + k + 3, attend, 0, unroll=3)
            if o == 0 and k == 0:
                poke(wa, w0, w1)

    def all_pairs(ref):
        return jnp.concatenate([ref[p] for p in range(PAIRS)], axis=1)

    for copy in loads[3:5]:
        copy.wait()

    def output_matrix():
        return jnp.concatenate(
            [
                beside(*(weights[o, 0, 3, k].reshape(HALF, HALF) for k in range(2)))
                for o in range(2)
            ],
            axis=0,
        )

    resid[...] = dot(all_pairs(mixed), output_matrix())

    def second_norm(rows):
        v = resid[rows] + stream[rows].astype(F32) + output_bias
        resid[rows] = v
        n, _ = norm_stats(v)
        normed_two[rows] = (n * second_gain + second_shift).astype(BF16)

    row_loop(second_norm)
    poke(w0, w1)

    for copy in loads[5:]:
        copy.wait()
    grad_resid[...] = jnp.zeros_like(grad_resid)
    dnorm[...] = jnp.zeros_like(dnorm)

    def feed(o, jj):
        small = small_mine if o == 0 else small_other
        bias = beside(small[pl.ds(3 + 2 * jj, 1)], small[pl.ds(4 + 2 * jj, 1)])
        w_expand = beside(slab(o, 1 + jj, 0), slab(o, 1 + jj, 1))
        hidden[...] = dot(normed_two[...], w_expand) + bias

        def gelu(rows):
            h = hidden[rows]
            big, slope_rows = phi_terms(h)
            block_low[rows] = (h * big).astype(BF16)
            hidden[rows] = slope_rows

        row_loop(gelu)
        w_reduce = beside(slab(o, 1 + jj, 2), slab(o, 1 + jj, 3))
        grad_resid[...] += dot(block_low[...], w_reduce)
        gh = (dot(go[...], w_reduce, NT) * hidden[...]).astype(BF16)
        grad_attended[...] = gh
        row = (8 + 2 * o + jj) * 8
        sums[pl.ds(row, 8)] = gh.astype(F32).reshape(-1, 8, WIDTH).sum(axis=0)
        dnorm[...] += dot(grad_attended[...], w_expand, NT)
        grad = dot(normed_two[...], grad_attended[...], TN).astype(BF16)
        keep_grad(grad, o, jj, 0)
        grad = dot(block_low[...], go[...], TN).astype(BF16)
        keep_grad(grad, o, jj, 2)

    def keep_grad(grad, o, jj, at):
        for k in range(2):
            grads[o, 1 + jj, at + k] = grad[:, k * HALF : (k + 1) * HALF].reshape(
                2, 4, 2, BLOCK, HALF
            )

    s0, s1 = (
        sum_steps(me, post, grads, theirs, bufs[g], total_out, own_sems.at[g], g) for g in (1, 2)
    )
    feed(0, 0)
    poke(s0, w0, w1)
    feed(0, 1)
    poke(s1)
    finish(w0, w1)
    feed(1, 0)
    poke(s0)
    feed(1, 1)
    poke(s1)

    for i in range(2):
        own = pl.ds(i * ROWS, ROWS)
        block_low[own] = ((resid[own] + grad_resid[own] + reduce_bias) * keep[i]).astype(BF16)
    block_store = pltpu.make_async_copy(block_low, block_out, own_sems.at[3])
    block_store.start()

    def norm_back(n, scale, grad, gain):
        e = grad * gain
        return scale * (
            e - jnp.mean(e, axis=-1, keepdims=True) - n * jnp.mean(e * n, axis=-1, keepdims=True)
        )

    def second_back(rows):
        n, scale = norm_stats(resid[rows])
        grad = dnorm[rows]
        total = go[rows].astype(F32)
        gather_sum(5, total)
        total = total + norm_back(n, scale, grad, second_gain)
        grad_resid[rows] = total
        low = total.astype(BF16)
        grad_attended[rows] = low
        gather_sum(2, grad * n)
        gather_sum(3, grad)
        gather_sum(4, low.astype(F32))

    row_loop(second_back)

    grad = dot(all_pairs(mixed), grad_attended[...], TN).astype(BF16)
    for o in range(2):
        for k in range(2):
            grads[o, 0, 3, k] = grad[
                o * HALF : (o + 1) * HALF, k * HALF : (k + 1) * HALF
            ].reshape(4, 2, BLOCK, HALF)
    sa = sum_steps(me, post, grads, theirs, bufs[0], total_out, own_sems.at[0], 0)
    poke(sa)
    result = dot(grad_attended[...], output_matrix(), NT).astype(BF16)
    for p in range(PAIRS):
        mixed[p] = result[:, 128 * p : 128 * (p + 1)]
    poke(s0, s1)

    def attend_back(k, carry):
        p, rows = lax.div(k, 2), image_rows(lax.rem(k, 2))
        grad_out = split(mixed[p, rows])
        soft_low = probs[k]
        soft = soft_low.astype(F32)
        grad_soft = dot(grad_out, qkv[2, p, rows], NT)
        inner = jnp.sum(soft * grad_soft, axis=-1, keepdims=True)
        grad_scores = (soft * (grad_soft - inner)).astype(BF16)
        scale = jnp.asarray(HD**-0.5, BF16)
        queries = split(qkv[0, p, rows] * scale)
        qkv[0, p, rows] = joined(dot(grad_scores, qkv[1, p, rows] * scale)).astype(BF16)
        qkv[1, p, rows] = dot(grad_scores, queries, TN).astype(BF16)
        qkv[2, p, rows] = dot(soft_low, grad_out, TN).astype(BF16)
        return carry

    for k in range(0, 12, 3):
        lax.fori_loop(k, k + 3, attend_back, 0, unroll=3)
    poke(s0, s1)

    for j in range(3):
        grad = dot(normed[...], all_pairs(qkv.at[j]), TN).astype(BF16)
        for o in range(2):
            grads[o, 0, j] = grad[:, o * HALF : (o + 1) * HALF].reshape(2, 4, 2, BLOCK, HALF)
        poke(sa)
    for j in range(3):
        given = all_pairs(qkv.at[j])
        back = dot(given, beside(slab(0, 0, j), slab(1, 0, j)), NT)
        if j == 0:
            dnorm[...] = back
        else:
            dnorm[...] += back
        if j != 1:
            row = 48 if j == 0 else 56
            sums[row : row + 8] = given.astype(F32).reshape(-1, 8, WIDTH).sum(axis=0)
        if j == 0:
            poke(sa, s0, s1)

    def first_back(rows):
        n, scale = norm_stats(stream[rows].astype(F32))
        grad = dnorm[rows]
        grad_resid[rows] = grad_resid[rows] + norm_back(n, scale, grad, first_gain)
        gather_sum(0, grad * n)
        gather_sum(1, grad)

    row_loop(first_back)
    input_store = pltpu.make_async_copy(grad_resid, input_grad, own_sems.at[4])
    input_store.start()

    totals = [jnp.sum(sums[8 * k : 8 * (k + 1)], axis=0, keepdims=True) for k in range(12)]

    def swapped(row):
        return jnp.where(first, row, jnp.concatenate([row[:, HALF:], row[:, :HALF]], axis=1))

    rows = totals[:6] + [swapped(totals[6]), swapped(totals[7])]
    for k in range(4):
        rows.append(jnp.where(first, totals[8 + k], totals[8 + (k + 2) % 4]))
    for k in range(12):
        acc[0, k : k + 1] = rows[k]
    acc[0, 12:16] = jnp.zeros((4, WIDTH), F32)
    sm = small_steps(me, post, acc, arrived)
    for _ in range(16):
        poke(sa, sm, s0, s1)
    finish(s0, s1, sm, sa)
    small_out[...] = acc[7]
    post.drain()
    block_store.wait()
    input_store.wait()


def layer(*operands):
    def buf(*shape, dtype=BF16):
        return pltpu.VMEM(shape, dtype)

    ring_bufs = [
        buf(*HELD[stage][third], THIRD, HALF)
        for group in range(GROUPS)
        for stage in range(3)
        for third in range(3)
    ]
    blocks = (3, 4, 2, 4, 2, BLOCK, HALF)
    return pl.pallas_call(
        layer_kernel,
        out_shape=(
            jax.ShapeDtypeStruct((BOTH, WIDTH), BF16),
            jax.ShapeDtypeStruct((BOTH, WIDTH), F32),
            jax.ShapeDtypeStruct(blocks, BF16),
            jax.ShapeDtypeStruct((16, WIDTH), F32),
        ),
        in_specs=[SMEM] + [VMEM] * 10 + [ANY] * 4,
        out_specs=(ANY, ANY, ANY, VMEM),
        scratch_shapes=[
            buf(2, *blocks),
            buf(2, *blocks),
            buf(2, 3, 4, 2, 4, BLOCK, HALF),
            *ring_bufs,
            buf(8, HALF, dtype=F32),
            buf(8, HALF, dtype=F32),
            buf(8, 16, WIDTH, dtype=F32),
            buf(7, 16, WIDTH, dtype=F32),
            buf(BOTH, WIDTH),
            buf(BOTH, WIDTH),
            buf(BOTH, WIDTH, dtype=F32),
            buf(BOTH, WIDTH, dtype=F32),
            buf(BOTH, WIDTH),
            buf(BOTH, WIDTH),
            buf(BOTH, WIDTH),
            buf(3, PAIRS, BOTH, 128),
            buf(PAIRS, BOTH, 128),
            buf(2 * PAIRS, 2 * ROWS, ROWS),
            buf(BOTH, WIDTH, dtype=F32),
            buf(BOTH, WIDTH, dtype=F32),
            buf(BOTH, WIDTH),
            buf(12 * 8, WIDTH, dtype=F32),
            pltpu.SemaphoreType.DMA((13,)),
            pltpu.SemaphoreType.DMA((5,)),
            pltpu.SemaphoreType.DMA((COPIES,)),
            pltpu.SemaphoreType.DMA((COPIES,)),
        ],
        compiler_params=pltpu.CompilerParams(
            collective_id=0, has_side_effects=True, vmem_limit_bytes=127 << 19
        ),
        name="layer",
    )(*operands)


def assemble_kernel(
    total, small, given, block, *rest
):
    (block_out, input_grad, project, output, expand, reduce, *vectors, project_bias, expand_bias) = (
        rest[:14]
    )
    low, full, load_sems, store_sems = rest[14:]
    loads, stores = [], []
    for group in range(GROUPS):
        for x in range(4):
            k = 4 * group + x
            copy = pltpu.make_async_copy(total.at[group, x], low.at[k], load_sems.at[k])
            copy.start()
            loads.append(copy)

    def store(src, dst):
        copy = pltpu.make_async_copy(src, dst, store_sems.at[len(stores)])
        copy.start()
        stores.append(copy)

    def columns(k):
        return pl.ds(k * HALF, HALF)

    for k, copy in enumerate(loads):
        copy.wait()

        def step(i, carry, k=k):
            rows = pl.ds(pl.multiple_of(i * BLOCK, BLOCK), BLOCK)
            zl, y, c = lax.div(i, 8), lax.rem(lax.div(i, 2), 4), lax.rem(i, 2)
            full[k, rows] = low[k, zl, y, c].astype(F32)
            return carry

        lax.fori_loop(0, 16, step, 0)
        group, x = divmod(k, 4)
        if group == 0 and x < 3:
            store(full.at[k], project.at[x])
        elif group == 0:
            for i in range(2):
                store(full.at[k, columns(i)], output.at[:, columns(i)])
        elif x < 2:
            store(full.at[k], expand.at[:, columns(2 * (group - 1) + x)])
        else:
            store(full.at[k], reduce.at[pl.ds((group - 1) * WIDTH, WIDTH), columns(x - 2)])
    for i in range(2):
        input_grad[:, i] = given[i * ROWS : i * ROWS + TOKENS]
    pair = [block[i * ROWS : i * ROWS + TOKENS] for i in range(2)]
    block_out[...] = jnp.stack(pair, axis=1)
    for k, ref in enumerate(vectors):
        ref[...] = small[k : k + 1].reshape(WIDTH)
    first = lax.axis_index("tensor") == 0
    project_bias[...] = jnp.where(first, small[6:8, :HALF], small[6:8, HALF:])
    for k in range(2):
        row = jnp.where(first, small[8 + k : 9 + k], small[10 + k : 11 + k])
        expand_bias[k * WIDTH : (k + 1) * WIDTH] = row.reshape(WIDTH)
    for copy in stores:
        copy.wait()


def assemble(*operands):
    def shape(*dims):
        return jax.ShapeDtypeStruct(dims, F32)

    return pl.pallas_call(
        assemble_kernel,
        out_shape=(
            jax.ShapeDtypeStruct((TOKENS, 2, WIDTH), BF16),
            shape(TOKENS, 2, WIDTH),
            shape(3, WIDTH, HALF),
            shape(HALF, WIDTH),
            shape(WIDTH, 4 * HALF),
            shape(4 * HALF, WIDTH),
            *[shape(WIDTH)] * 6,
            shape(2, HALF),
            shape(4 * HALF),
        ),
        in_specs=[ANY, VMEM, VMEM, VMEM],
        out_specs=(VMEM, VMEM, *[ANY] * 4, *[VMEM] * 8),
        scratch_shapes=[
            pltpu.VMEM((12, 2, 4, 2, BLOCK, HALF), BF16),
            pltpu.VMEM((12, WIDTH, HALF), F32),
            pltpu.SemaphoreType.DMA((12,)),
            pltpu.SemaphoreType.DMA((13,)),
        ],
        compiler_params=pltpu.CompilerParams(vmem_limit_bytes=60 << 20),
        name="assemble",
    )(*operands)


def shards(
    inputs,
    image_counts,
    first_gain,
    first_shift,
    project_weight,
    project_bias,
    output_weight,
    output_bias,
    second_gain,
    second_shift,
    expand_weight,
    expand_bias,
    reduce_weight,
    reduce_bias,
    out_cotangent,
):
    block_out, input_grad, total, small_total = layer(
        image_counts,
        jnp.transpose(inputs, (1, 0, 2)),
        jnp.transpose(out_cotangent, (1, 0, 2)),
        first_gain,
        first_shift,
        second_gain,
        second_shift,
        output_bias,
        reduce_bias,
        project_bias,
        expand_bias,
        jnp.transpose(project_weight, (1, 0, 2)).reshape(3, 2, 4, 2, BLOCK, HALF),
        output_weight.reshape(4, 2, BLOCK, WIDTH),
        expand_weight.reshape(2, 4, 2, BLOCK, 4 * HALF),
        reduce_weight.reshape(2, 2, 4, 2, BLOCK, WIDTH),
    )
    block_out, input_grad, project, output, expand, reduce, *vectors, bias, feed_bias = assemble(
        total, small_total, input_grad, block_out
    )
    return (
        jnp.transpose(block_out, (1, 0, 2)),
        jnp.transpose(input_grad, (1, 0, 2)),
        vectors[0],
        vectors[1],
        jnp.transpose(project, (1, 0, 2)),
        bias,
        output,
        vectors[4],
        vectors[2],
        vectors[3],
        expand,
        feed_bias,
        reduce,
        vectors[5],
    )


def solution(mesh):
    in_specs = (
        P(("dp", "tensor"), None, None),
        P("dp"),
        P(),
        P(),
        P(None, None, "tensor"),
        P(None, "tensor"),
        P("tensor", None),
        P(),
        P(),
        P(),
        P(None, "tensor"),
        P("tensor"),
        P("tensor", None),
        P(),
        P(("dp", "tensor"), None, None),
    )
    out_specs = (
        P(("dp", "tensor"), None, None),
        P(("dp", "tensor"), None, None),
        P(),
        P(),
        P(None, None, "tensor"),
        P(None, "tensor"),
        P("tensor", None),
        P(),
        P(),
        P(),
        P(None, "tensor"),
        P("tensor"),
        P("tensor", None),
        P(),
    )
    return jax.shard_map(shards, mesh=mesh, in_specs=in_specs, out_specs=out_specs, check_vma=False)
```
